32 devices in a mesh: lat: 16 (over z, y, core), lev: 2 (over x).
Axes of the slice: x: 2, y: 2, z: 4, core: 2. Of those that a mesh axis runs over, the one named last changes fastest.
Arguments:
- spectral_in: bfloat16 [2, 336, 2, 1280], P('lev', 'lat'), may hold values from -0.25 to 0.25
- legendre: bfloat16 [2, 336, 640, 32], P('lev', 'lat'), may hold values from -0.25 to 0.25
- slot_wave: int32 [2, 336], replicated, may hold values from 0 to 640, as said below
- row_length: int32 [32], P('lat'), may hold values from 16 to 2688, as said below
- quad_weight: float32 [32], replicated, may hold values from 8 to 64
Outputs:
- grid_field: bfloat16 [2, 32, 2688], P('lev', 'lat')
- spectral_out: bfloat16 [2, 336, 2, 1280], P('lev', 'lat')
The draws below stay inside these ranges and needn't reach their ends.
Inputs may be any that keep to these rules, and one draw needn't show every extreme that they name: `slot_wave`: each wavenumber 0 to 639 stands in exactly one slot; all other slots hold 640. Each device holds at most 21 of the wavenumbers. `row_length`: lengths are multiples of 4; the two middle rows have length 2688.
All inputs are finite; a program needn't handle non-finite values.
Results may differ from the reference program's by a relative error of at most 0.0072.
Values may be sent and summed in bfloat16 or wider, within the bound.
A program may use at most 64 MiB of HBM per device.

```python
import math
import jax
import jax.numpy as jnp
from jax import lax

M = 640
NDEG = 640
NLON = 2688
NLAT = 32
FIELDS = 2
OWN_LAT = 21
OWN = 336
N_LAT = 16
N_LEV = 2


def draw_slot_wave(key, part):
    key = jax.random.fold_in(key, 11)
    first_key, second_key = jax.random.split(key)
    total_slots = N_LEV * OWN
    slot_index = jnp.arange(total_slots, dtype=jnp.int32)
    owner_device = slot_index // OWN * N_LAT + slot_index % OWN // OWN_LAT
    ranks = jax.random.permutation(first_key, total_slots).astype(jnp.int32)
    busiest = jax.random.randint(second_key, (), 0, N_LEV * N_LAT, dtype=jnp.int32)
    scores = ranks - jnp.where(owner_device == busiest, total_slots, 0).astype(jnp.int32)
    ordering = jnp.argsort(scores, stable=True).astype(jnp.int32)
    wave_ids = jnp.full((total_slots,), M, dtype=jnp.int32)
    wave_ids = wave_ids.at[ordering[:M]].set(jnp.arange(M, dtype=jnp.int32))
    return wave_ids.reshape(N_LEV, OWN)


def draw_row_length(key, part):
    key = jax.random.fold_in(key, 23)
    row_index = jnp.arange(NLAT, dtype=jnp.int32)
    distance = jnp.minimum(row_index, NLAT - 1 - row_index)
    half_count = NLAT // 2
    base_length = 16 + 4 * ((NLON - 16) // 4 * (distance + 1) // half_count)
    jitter = 4 * jax.random.randint(key, (NLAT,), 0, 4, dtype=jnp.int32)
    length = jnp.where(distance == half_count - 1, NLON, jnp.maximum(base_length - jitter, 16))
    return length.astype(jnp.int32)


def block_scale(own_key, extent, cuts, smallest, high):
    def one(dim, shards_of):
        heights = jax.random.uniform(jax.random.fold_in(jax.random.fold_in(own_key, 6), dim), (shards_of,), jnp.float32, smallest / len(cuts), high / len(cuts))
        return jnp.repeat(jnp.exp(heights), extent[dim] // shards_of).reshape((-1,) + (1,) * (len(extent) - dim - 1))

    factor_of = one(*cuts[0])
    for cut in cuts[1:]:
        factor_of = factor_of * one(*cut)
    return factor_of


def noise(own_key, dims, width, limit, cuts=(), held_as=jnp.bfloat16):
    loudness = block_scale(own_key, dims, cuts, -0.22, 0.18) if cuts else 1.0
    array = jax.random.normal(own_key, dims, jnp.float32) * width * loudness
    return jnp.minimum(jnp.maximum(array, -limit), limit).astype(held_as)


def setup_inputs(seed: int = 0) -> dict:
    key_of = jax.random.split(jax.random.key(seed), 6)
    return {
        "spectral_in": noise(key_of[0], (N_LEV, OWN, FIELDS, 2 * NDEG), 0.04, 0.25, ((0, 2), (1, 16))),
        "legendre": noise(key_of[1], (N_LEV, OWN, NDEG, NLAT), NDEG ** -0.5, 0.25, ((0, 2), (1, 16))),
        "slot_wave": draw_slot_wave(jax.random.fold_in(key_of[5], 71), 0),
        "row_length": draw_row_length(jax.random.fold_in(key_of[5], 71), 0),
        "quad_weight": jnp.clip(jnp.exp(jax.random.uniform(key_of[4], (NLAT,), jnp.float32, math.log(8.0), math.log(64.0))), 8.0, 64.0),
    }


def transform_row(coeffs_row, length, wave_ids):
    lon_index = jnp.arange(NLON, dtype=jnp.int32)
    phase_turn = (wave_ids[:, None] * lon_index[None, :]) % length
    step_angle = (2.0 * math.pi) / length.astype(jnp.float32)
    angles = phase_turn.astype(jnp.float32) * step_angle
    inside = (lon_index[None, :] < length) & (wave_ids[:, None] < M)
    dft_table = jnp.concatenate([jnp.where(inside, jnp.cos(angles), 0.0), jnp.where(inside, jnp.sin(angles), 0.0)], 0).astype(jnp.bfloat16)
    factor = jnp.where(wave_ids == 0, 1.0, 2.0).astype(jnp.bfloat16)
    stacked = jnp.concatenate([coeffs_row[:, :, 0] * factor[:, None], -(coeffs_row[:, :, 1] * factor[:, None])], 0)
    grid_raw = jnp.dot(stacked.T, dft_table, preferred_element_type=jnp.float32)
    shaped = (grid_raw * (1.0 + 0.5 * jnp.tanh(grid_raw))).astype(jnp.bfloat16)
    summed = jnp.dot(shaped, dft_table.T, preferred_element_type=jnp.float32)
    slot_count = wave_ids.shape[0]
    length_float = length.astype(jnp.float32)
    real_back = summed[:, :slot_count] / length_float
    imag_back = -summed[:, slot_count:] / length_float
    four_row = jnp.stack([real_back, imag_back], -1).astype(jnp.bfloat16)
    return shaped, jnp.transpose(four_row, (1, 0, 2))


def reference(spectral_in, legendre, slot_wave, row_length, quad_weight):
    wave_ids = slot_wave.reshape(-1)
    slot_count = wave_ids.shape[0]
    keep_mask = (jnp.arange(NDEG, dtype=jnp.int32)[None, :] >= wave_ids[:, None]).astype(jnp.bfloat16)
    coeffs = spectral_in.reshape(slot_count, FIELDS, 2, NDEG) * keep_mask[:, None, None, :]
    coeffs = coeffs.reshape(slot_count, FIELDS * 2, NDEG)
    matrices = legendre.reshape(slot_count, NDEG, NLAT)

    def inverse_slot(packed):
        return jnp.dot(packed[0], packed[1], preferred_element_type=jnp.float32).astype(jnp.bfloat16)

    fourier = lax.map(inverse_slot, (coeffs, matrices))
    four_rows = jnp.transpose(fourier.reshape(slot_count, FIELDS, 2, NLAT), (3, 0, 1, 2))

    def one_row(packed):
        return transform_row(packed[0], packed[1], wave_ids)

    shaped_rows, four_out = lax.map(one_row, (four_rows, row_length))
    grid_field = jnp.transpose(shaped_rows, (1, 0, 2))
    weighted = (four_out * quad_weight[:, None, None, None]).astype(jnp.bfloat16)
    weighted = jnp.transpose(weighted.reshape(NLAT, slot_count, FIELDS * 2), (1, 2, 0))

    def direct_slot(packed):
        return jnp.dot(packed[0], packed[1].T, preferred_element_type=jnp.float32)

    direct = lax.map(direct_slot, (weighted, matrices)) * keep_mask[:, None, :].astype(jnp.float32)
    spectral_out = direct.reshape(N_LEV, OWN, FIELDS, 2 * NDEG).astype(jnp.bfloat16)
    return grid_field, spectral_out
```

```python
import functools

import jax
import jax.numpy as jnp
from jax import lax
from jax.experimental import pallas as pl
from jax.experimental.pallas import tpu as pltpu
from jax.sharding import PartitionSpec as P

M = 640
NLON = 2688
LOW = 32
HIGH = 24
STEP = 384
GROUP = 8
F32 = jnp.float32
BF16 = jnp.bfloat16

SIN = (3.1415927410125732, -5.167709827423096, 2.550076961517334, -0.5982866883277893, 0.07764717191457748)
COS = (1.0, -4.934802055358887, 4.058709144592285, -1.3352116346359253, 0.234935462474823, -0.024393025785684586)


def horner(coefs, x):
    total = jnp.full_like(x, coefs[-1])
    for c in coefs[-2::-1]:
        total = total * x + c
    return total


def turn_cos_sin(product, length):
    inverse = 1.0 / length
    rest = product - jnp.round(product * inverse) * length
    t = rest * inverse
    square = t * t
    half_sin = t * horner(SIN, square)
    half_cos = horner(COS, square)
    return 1.0 - 2.0 * half_sin * half_sin, 2.0 * half_sin * half_cos


def dot_nn(a, b):
    return lax.dot_general(a, b, (((1,), (0,)), ((), ())), preferred_element_type=F32)


def dot_nt(a, b):
    return lax.dot_general(a, b, (((1,), (1,)), ((), ())), preferred_element_type=F32)


def split(x):
    high = x.astype(BF16)
    return high, (x - high.astype(F32)).astype(BF16)


def kernel(
    n_lat, n_lev, wave_ref, length_ref, quad_ref, spec_ref, leg_ref, grid_ref, out_ref,
    four, stacked, send1, recv1, send2, recv2, columns, flipped, table_p, table_q, table_b, sems,
):
    n = n_lat * n_lev
    lat = lax.axis_index("lat")
    lev = lax.axis_index("lev")
    me = lev * n_lat + lat
    own, fields = spec_ref.shape[0], spec_ref.shape[1]
    rows, deg = leg_ref.shape[1], leg_ref.shape[2]
    local = length_ref.shape[0]
    per_slot = 2 * fields

    def partner(t):
        other = lax.rem(me + t, n)
        return other, (lax.rem(other, n_lat), lax.div(other, n_lat))

    barrier = pltpu.get_barrier_semaphore()

    def greet(t, carry):
        pl.semaphore_signal(barrier, inc=1, device_id=partner(t)[1], device_id_type=pl.DeviceIdType.MESH)
        return carry

    lax.fori_loop(1, n, greet, 0)

    degree = lax.broadcasted_iota(jnp.int32, (per_slot, deg), 1)
    lane = lax.broadcasted_iota(jnp.int32, (1, 128), 1)
    wave_row = jnp.full((1, 128), float(M), F32)
    four[...] = jnp.zeros_like(four)
    for s in range(own):
        m = wave_ref[lev, lat * own + s]
        x = spec_ref[s].astype(F32)
        x = jnp.concatenate([x[:, :deg], x[:, deg:]], 0)
        x = jnp.where(degree >= m, x, 0.0).astype(BF16)
        four[pl.ds(s * per_slot, per_slot), pl.ds(0, rows)] = dot_nt(x, leg_ref[s]).astype(BF16).astype(F32)
        wave_row = jnp.where(lane // per_slot == s, m.astype(F32), wave_row)
    turned = four[...].T
    for j in range(n_lat):
        send1[j, pl.ds(0, local), :] = turned[j * local : (j + 1) * local, :]
        send1[j, pl.ds(local, 1), :] = wave_row
        send1[j, pl.ds(local + 1, send1.shape[1] - local - 1), :] = jnp.zeros(
            (send1.shape[1] - local - 1, 128), F32
        )

    pl.semaphore_wait(barrier, n - 1)

    def remote(src, dst, k, device):
        return pltpu.make_async_remote_copy(
            src_ref=src, dst_ref=dst, send_sem=sems.at[2 * k], recv_sem=sems.at[2 * k + 1],
            device_id=device, device_id_type=pl.DeviceIdType.MESH,
        )

    def send_rows(t, carry):
        _, device = partner(t)
        remote(send1.at[device[0]], recv1.at[me], 0, device).start()
        return carry

    lax.fori_loop(1, n, send_rows, 0)
    recv1[me] = send1[lat]

    for r in range(local):
        length = jnp.full((1, STEP), length_ref[r].astype(F32), F32)

        def tables(i, carry):
            at = pl.multiple_of(i * STEP, 128)
            k = (lax.broadcasted_iota(jnp.int32, (1, STEP), 1) + at).astype(F32)
            a = lax.broadcasted_iota(jnp.int32, (HIGH, STEP), 0).astype(F32) * float(LOW)
            cos_a, sin_a = turn_cos_sin(a * k, length)
            p = jnp.concatenate([cos_a, -sin_a], 0)
            q = jnp.concatenate([sin_a, cos_a], 0)
            table_p[r, :, pl.ds(at, STEP)] = jnp.concatenate(split(p), 0)
            table_q[r, :, pl.ds(at, STEP)] = jnp.concatenate(split(q), 0)
            b = lax.broadcasted_iota(jnp.int32, (LOW, STEP), 0).astype(F32)
            cos_b, sin_b = turn_cos_sin(b * k, length)
            table_b[r, :, pl.ds(at, STEP)] = jnp.concatenate([cos_b, sin_b], 0)
            return carry

        lax.fori_loop(0, NLON // STEP, tables, 0)

    def all_arrived(buffer, k):
        part = buffer.at[pl.ds(0, n - 1)]
        pltpu.make_async_copy(part, part, sems.at[k]).wait()

    all_arrived(recv1, 1)

    index_a = lax.broadcasted_iota(jnp.int32, (HIGH, 128), 0)
    index_b = lax.broadcasted_iota(jnp.int32, (LOW, 128), 0)
    is_real = lax.rem(lane, per_slot) == lev
    is_imag = lax.rem(lane, per_slot) == lev + fields

    def one_hots(o):
        w = recv1[o, pl.ds(local, 1), :].astype(jnp.int32)
        return index_a == w // LOW, (index_b == w % LOW).astype(F32)

    def place(g, totals):
        lefts = []
        rights = [[] for _ in range(local)]
        for i in range(GROUP):
            o = g * GROUP + i
            hot_a, hot_b = one_hots(o)
            lefts.append(hot_b)
            for r in range(local):
                z = recv1[o, pl.ds(r, 1), :]
                pieces = [
                    jnp.where(hot_a, jnp.where(which, z, 0.0), 0.0) for which in (is_real, is_imag)
                ]
                rights[r].append(jnp.concatenate(pieces, 0))
        left = jnp.concatenate(lefts, 1).astype(BF16)
        return tuple(
            totals[r] + dot_nt(left, jnp.concatenate(rights[r], 1).astype(BF16)) for r in range(local)
        )

    placed = lax.fori_loop(
        0, n // GROUP, place, tuple(jnp.zeros((LOW, 2 * HIGH), F32) for _ in range(local))
    )

    row_b = lax.broadcasted_iota(jnp.int32, (LOW, 2 * HIGH), 0)
    col_a = lax.rem(lax.broadcasted_iota(jnp.int32, (LOW, 2 * HIGH), 1), HIGH)
    factor = jnp.where((row_b == 0) & (col_a == 0), 1.0, 2.0)
    spectra = []
    for r in range(local):
        z = placed[r] * factor
        z = jnp.concatenate([z, z], 1).astype(BF16)
        length_int = length_ref[r]

        def longitudes(i, total):
            at = pl.multiple_of(i * STEP, 128)
            here = pl.ds(at, STEP)
            cos_b = table_b[r, pl.ds(0, LOW), here]
            sin_b = table_b[r, pl.ds(LOW, LOW), here]
            q = table_q[r, :, here]
            raw = jnp.sum(
                dot_nn(z, table_p[r, :, here]) * cos_b - dot_nn(z, q) * sin_b, axis=0, keepdims=True
            )
            shaped = (raw * (1.0 + 0.5 * jnp.tanh(raw))).astype(BF16).astype(F32)
            k = lax.broadcasted_iota(jnp.int32, (1, STEP), 1) + at
            shaped = jnp.where(k < length_int, shaped, 0.0)
            columns[pl.ds(r, 1), here] = shaped
            g = jnp.concatenate([shaped * cos_b, shaped * sin_b], 0)
            return total + dot_nt(q, jnp.concatenate(split(g), 0))

        total = lax.fori_loop(
            0, NLON // STEP, longitudes, jnp.zeros((4 * HIGH, 4 * LOW), F32)
        )
        both = 2 * HIGH
        total = total[:both, : 2 * LOW] + total[both:, : 2 * LOW] + total[:both, 2 * LOW :]
        ss, sc = total[:HIGH, LOW:], total[:HIGH, :LOW]
        cs, cc = total[HIGH:, LOW:], total[HIGH:, :LOW]
        length = jnp.full((HIGH, LOW), length_int.astype(F32), F32)
        weight = quad_ref[lat * local + r]
        for part in (cc - ss, -(sc + cs)):
            spectra.append((part / length).astype(BF16).astype(F32) * weight)
    grid_ref[...] = columns[pl.ds(0, local), :].astype(BF16)
    spectrum = jnp.concatenate(spectra, 0).astype(BF16)

    def pick(g, carry):
        hots = [one_hots(g * GROUP + i) for i in range(GROUP)]
        right = jnp.concatenate([hot_b for _, hot_b in hots], 1).astype(BF16)
        spread = dot_nn(spectrum, right)
        for i in range(GROUP):
            cut = spread[:, i * 128 : (i + 1) * 128]
            lines = []
            for r in range(local):
                line = jnp.zeros((1, 128), F32)
                for c, which in enumerate((is_real, is_imag)):
                    first = (2 * r + c) * HIGH
                    value = jnp.sum(
                        jnp.where(hots[i][0], cut[first : first + HIGH], 0.0), axis=0, keepdims=True
                    )
                    line = jnp.where(which, value, line)
                lines.append(line)
            send2[g * GROUP + i] = jnp.concatenate(lines, 0)
        return carry

    lax.fori_loop(0, n // GROUP, pick, 0)

    def send_slots(t, carry):
        other, device = partner(t)
        remote(send2.at[other], recv2.at[me], 1, device).start()
        return carry

    lax.fori_loop(1, n, send_slots, 0)
    recv2[me] = send2[me]
    all_arrived(recv2, 3)

    for j in range(n_lat):
        value = recv2[j]
        for g in range(1, n_lev):
            value = value + recv2[g * n_lat + j]
        stacked[pl.ds(j * local, local), :] = value
    flipped[...] = stacked[...].T
    for s in range(own):
        m = wave_ref[lev, lat * own + s]
        w = flipped[pl.ds(s * per_slot, per_slot), :].astype(BF16)
        y = jnp.where(degree >= m, dot_nn(w, leg_ref[s]), 0.0)
        out_ref[s] = jnp.concatenate([y[:fields], y[fields:]], 1).astype(BF16)

    all_arrived(recv1, 0)
    all_arrived(recv2, 2)


def shards(n_lat, n_lev, spectral_in, legendre, slot_wave, row_length, quad_weight):
    _, own, fields, double = spectral_in.shape
    _, _, deg, rows = legendre.shape
    local = row_length.shape[0]
    n = n_lat * n_lev
    assert fields == n_lev and own * fields * 2 <= 128 and n % GROUP == 0 and rows % 8 == 0
    rows_up = -(-rows // 128) * 128
    message = 4 if local < 4 else -(-(local + 1) // 8) * 8
    vmem = pl.BlockSpec(memory_space=pltpu.VMEM)
    smem = pl.BlockSpec(memory_space=pltpu.SMEM)
    grid, out = pl.pallas_call(
        functools.partial(kernel, n_lat, n_lev),
        out_shape=(
            jax.ShapeDtypeStruct((local, NLON), BF16),
            jax.ShapeDtypeStruct((own, fields, double), BF16),
        ),
        in_specs=[smem, smem, smem, vmem, vmem],
        out_specs=(vmem, vmem),
        scratch_shapes=[
            pltpu.VMEM((128, rows_up), F32),
            pltpu.VMEM((rows, 128), F32),
            pltpu.VMEM((n_lat, message, 128), F32),
            pltpu.VMEM((n, message, 128), F32),
            pltpu.VMEM((n, local, 128), F32),
            pltpu.VMEM((n, local, 128), F32),
            pltpu.VMEM((8, NLON), F32),
            pltpu.VMEM((128, rows), F32),
            pltpu.VMEM((local, 4 * HIGH, NLON), BF16),
            pltpu.VMEM((local, 4 * HIGH, NLON), BF16),
            pltpu.VMEM((local, 2 * LOW, NLON), F32),
            pltpu.SemaphoreType.DMA((4,)),
        ],
        compiler_params=pltpu.CompilerParams(
            collective_id=0, has_side_effects=True, vmem_limit_bytes=48 * 1024 * 1024
        ),
    )(
        slot_wave, row_length, quad_weight, spectral_in.reshape(own, fields, double),
        jnp.transpose(legendre.reshape(own, deg, rows), (0, 2, 1)),
    )
    return grid[None], out[None]


def solution(mesh):
    in_specs = (P("lev", "lat", None, None), P("lev", "lat", None, None), P(), P("lat"), P())
    out_specs = (P("lev", "lat", None), P("lev", "lat", None, None))
    body = functools.partial(shards, mesh.shape["lat"], mesh.shape["lev"])
    return jax.shard_map(body, mesh=mesh, in_specs=in_specs, out_specs=out_specs, check_vma=False)
```

```python
import functools

import jax
import jax.numpy as jnp
from jax import lax
from jax.experimental import pallas as pl
from jax.experimental.pallas import tpu as pltpu
from jax.sharding import PartitionSpec as P

M = 640
NLON = 2688
LOW = 32
HIGH = 24
STEP = 896
GROUP = 32
F32 = jnp.float32
BF16 = jnp.bfloat16

SIN = (3.1415927410125732, -5.167709827423096, 2.550076961517334, -0.5982866883277893, 0.07764717191457748)
COS = (1.0, -4.934802055358887, 4.058709144592285, -1.3352116346359253, 0.234935462474823, -0.024393025785684586)


def horner(coefs, x):
    total = jnp.full_like(x, coefs[-1])
    for c in coefs[-2::-1]:
        total = total * x + c
    return total


def turn_cos_sin(product, length):
    inverse = 1.0 / length
    rest = product - jnp.round(product * inverse) * length
    t = rest * inverse
    square = t * t
    half_sin = t * horner(SIN, square)
    half_cos = horner(COS, square)
    return 1.0 - 2.0 * half_sin * half_sin, 2.0 * half_sin * half_cos


def dot_nn(a, b):
    return lax.dot_general(a, b, (((1,), (0,)), ((), ())), preferred_element_type=F32)


def dot_nt(a, b):
    return lax.dot_general(a, b, (((1,), (1,)), ((), ())), preferred_element_type=F32)


def split(x):
    high = x.astype(BF16)
    return high, (x - high.astype(F32)).astype(BF16)


def kernel(
    n_lat, n_lev, wave_in, length_in, quad_in, spec_in, leg_in, grid_ref, out_ref,
    wave_ref, length_ref, quad_ref, spec_ref, leg_ref, load_sems, four, stacked, send1, recv1, send2, recv2, columns, flipped, table_p, table_q, table_b, sems,
):
    n = n_lat * n_lev
    lat = lax.axis_index("lat")
    lev = lax.axis_index("lev")
    me = lev * n_lat + lat
    own, fields = spec_ref.shape[0], spec_ref.shape[1]
    rows, deg = leg_ref.shape[1], leg_ref.shape[2]
    local = length_ref.shape[0]
    per_slot = 2 * fields

    def partner(t):
        other = lax.rem(me + t, n)
        return other, (lax.rem(other, n_lat), lax.div(other, n_lat))

    pairs = (
        (spec_in, spec_ref), (leg_in, leg_ref), (wave_in, wave_ref), (length_in, length_ref), (quad_in, quad_ref),
    )
    loads = [pltpu.make_async_copy(src, dst, load_sems.at[i]) for i, (src, dst) in enumerate(pairs)]
    for load in loads:
        load.start()

    barrier = pltpu.get_barrier_semaphore()

    def greet(t, carry):
        pl.semaphore_signal(barrier, inc=1, device_id=partner(t)[1], device_id_type=pl.DeviceIdType.MESH)
        return carry

    lax.fori_loop(1, n, greet, 0)

    degree = lax.broadcasted_iota(jnp.int32, (per_slot, deg), 1)
    lane = lax.broadcasted_iota(jnp.int32, (1, 128), 1)
    wave_row = jnp.full((1, 128), float(M), F32)
    four[...] = jnp.zeros_like(four)
    for load in loads:
        load.wait()
    for s in range(own):
        m = wave_ref[lev, lat * own + s]
        x = spec_ref[s].astype(F32)
        x = jnp.concatenate([x[:, :deg], x[:, deg:]], 0)
        x = jnp.where(degree >= m, x, 0.0).astype(BF16)
        four[pl.ds(s * per_slot, per_slot), pl.ds(0, rows)] = dot_nt(x, leg_ref[s]).astype(BF16).astype(F32)
        wave_row = jnp.where(lane // per_slot == s, m.astype(F32), wave_row)
    turned = four[...].T
    for j in range(n_lat):
        send1[j, pl.ds(0, local), :] = turned[j * local : (j + 1) * local, :]
        send1[j, pl.ds(local, 1), :] = wave_row
        send1[j, pl.ds(local + 1, send1.shape[1] - local - 1), :] = jnp.zeros(
            (send1.shape[1] - local - 1, 128), F32
        )

    pl.semaphore_wait(barrier, n - 1)

    def remote(src, dst, k, device):
        return pltpu.make_async_remote_copy(
            src_ref=src, dst_ref=dst, send_sem=sems.at[2 * k], recv_sem=sems.at[2 * k + 1],
            device_id=device, device_id_type=pl.DeviceIdType.MESH,
        )

    def send_rows(t, carry):
        _, device = partner(t)
        remote(send1.at[device[0]], recv1.at[me], 0, device).start()
        return carry

    lax.fori_loop(1, n, send_rows, 0)
    recv1[me] = send1[lat]

    for r in range(local):
        length = jnp.full((1, STEP), length_ref[r].astype(F32), F32)

        for at in range(0, NLON, STEP):
            k = (lax.broadcasted_iota(jnp.int32, (1, STEP), 1) + at).astype(F32)
            a = lax.broadcasted_iota(jnp.int32, (HIGH, STEP), 0).astype(F32) * float(LOW)
            cos_a, sin_a = turn_cos_sin(a * k, length)
            p = jnp.concatenate([cos_a, -sin_a], 0)
            q = jnp.concatenate([sin_a, cos_a], 0)
            table_p[r, :, pl.ds(at, STEP)] = jnp.concatenate(split(p), 0)
            table_q[r, :, pl.ds(at, STEP)] = jnp.concatenate(split(q), 0)
            b = lax.broadcasted_iota(jnp.int32, (LOW, STEP), 0).astype(F32)
            cos_b, sin_b = turn_cos_sin(b * k, length)
            table_b[r, :, pl.ds(at, STEP)] = jnp.concatenate([cos_b, sin_b], 0)

    def all_arrived(buffer, k):
        part = buffer.at[pl.ds(0, n - 1)]
        pltpu.make_async_copy(part, part, sems.at[k]).wait()

    all_arrived(recv1, 1)

    index_a = lax.broadcasted_iota(jnp.int32, (HIGH, 128), 0)
    index_b = lax.broadcasted_iota(jnp.int32, (LOW, 128), 0)
    is_real = lax.rem(lane, per_slot) == lev
    is_imag = lax.rem(lane, per_slot) == lev + fields

    def one_hots(o):
        w = recv1[o, pl.ds(local, 1), :].astype(jnp.int32)
        return index_a == w // LOW, (index_b == w % LOW).astype(F32)

    def place(g, totals):
        lefts = []
        rights = [[] for _ in range(local)]
        for i in range(GROUP):
            o = g * GROUP + i
            hot_a, hot_b = one_hots(o)
            lefts.append(hot_b)
            for r in range(local):
                z = recv1[o, pl.ds(r, 1), :]
                pieces = [
                    jnp.where(hot_a, jnp.where(which, z, 0.0), 0.0) for which in (is_real, is_imag)
                ]
                rights[r].append(jnp.concatenate(pieces, 0))
        left = jnp.concatenate(lefts, 1).astype(BF16)
        return tuple(
            totals[r] + dot_nt(left, jnp.concatenate(rights[r], 1).astype(BF16)) for r in range(local)
        )

    placed = tuple(jnp.zeros((LOW, 2 * HIGH), F32) for _ in range(local))
    placed = place(0, placed) if n == GROUP else lax.fori_loop(0, n // GROUP, place, placed)

    row_b = lax.broadcasted_iota(jnp.int32, (LOW, 2 * HIGH), 0)
    col_a = lax.rem(lax.broadcasted_iota(jnp.int32, (LOW, 2 * HIGH), 1), HIGH)
    factor = jnp.where((row_b == 0) & (col_a == 0), 1.0, 2.0)
    spectra = []
    for r in range(local):
        z = placed[r] * factor
        z = jnp.concatenate([z, z], 1).astype(BF16)
        length_int = length_ref[r]

        total = jnp.zeros((4 * HIGH, 4 * LOW), F32)
        for at in range(0, NLON, STEP):
            here = pl.ds(at, STEP)
            cos_b = table_b[r, pl.ds(0, LOW), here]
            sin_b = table_b[r, pl.ds(LOW, LOW), here]
            q = table_q[r, :, here]
            raw = jnp.sum(
                dot_nn(z, table_p[r, :, here]) * cos_b - dot_nn(z, q) * sin_b, axis=0, keepdims=True
            )
            shaped = (raw * (1.0 + 0.5 * jnp.tanh(raw))).astype(BF16).astype(F32)
            k = lax.broadcasted_iota(jnp.int32, (1, STEP), 1) + at
            shaped = jnp.where(k < length_int, shaped, 0.0)
            columns[pl.ds(r, 1), here] = shaped
            g = jnp.concatenate([shaped * cos_b, shaped * sin_b], 0)
            total = total + dot_nt(q, jnp.concatenate(split(g), 0))
        both = 2 * HIGH
        total = total[:both, : 2 * LOW] + total[both:, : 2 * LOW] + total[:both, 2 * LOW :]
        ss, sc = total[:HIGH, LOW:], total[:HIGH, :LOW]
        cs, cc = total[HIGH:, LOW:], total[HIGH:, :LOW]
        length = jnp.full((HIGH, LOW), length_int.astype(F32), F32)
        weight = quad_ref[lat * local + r]
        for part in (cc - ss, -(sc + cs)):
            spectra.append((part / length).astype(BF16).astype(F32) * weight)
    grid_ref[...] = columns[pl.ds(0, local), :].astype(BF16)
    spectrum = jnp.concatenate(spectra, 0).astype(BF16)

    def pick(g, carry):
        hots = [one_hots(g * GROUP + i) for i in range(GROUP)]
        right = jnp.concatenate([hot_b for _, hot_b in hots], 1).astype(BF16)
        spread = dot_nn(spectrum, right)
        for i in range(GROUP):
            cut = spread[:, i * 128 : (i + 1) * 128]
            lines = []
            for r in range(local):
                line = jnp.zeros((1, 128), F32)
                for c, which in enumerate((is_real, is_imag)):
                    first = (2 * r + c) * HIGH
                    value = jnp.sum(
                        jnp.where(hots[i][0], cut[first : first + HIGH], 0.0), axis=0, keepdims=True
                    )
                    line = jnp.where(which, value, line)
                lines.append(line)
            send2[g * GROUP + i] = jnp.concatenate(lines, 0)
        return carry

    if n == GROUP:
        pick(0, 0)
    else:
        lax.fori_loop(0, n // GROUP, pick, 0)

    def send_slots(t, carry):
        other, device = partner(t)
        remote(send2.at[other], recv2.at[me], 1, device).start()
        return carry

    lax.fori_loop(1, n, send_slots, 0)
    recv2[me] = send2[me]
    all_arrived(recv2, 3)

    for j in range(n_lat):
        value = recv2[j]
        for g in range(1, n_lev):
            value = value + recv2[g * n_lat + j]
        stacked[pl.ds(j * local, local), :] = value
    flipped[...] = stacked[...].T
    for s in range(own):
        m = wave_ref[lev, lat * own + s]
        w = flipped[pl.ds(s * per_slot, per_slot), :].astype(BF16)
        y = jnp.where(degree >= m, dot_nn(w, leg_ref[s]), 0.0)
        out_ref[s] = jnp.concatenate([y[:fields], y[fields:]], 1).astype(BF16)

    all_arrived(recv1, 0)
    all_arrived(recv2, 2)


def shards(n_lat, n_lev, spectral_in, legendre, slot_wave, row_length, quad_weight):
    _, own, fields, double = spectral_in.shape
    _, _, deg, rows = legendre.shape
    local = row_length.shape[0]
    n = n_lat * n_lev
    assert fields == n_lev and own * fields * 2 <= 128 and n % GROUP == 0 and rows % 8 == 0
    rows_up = -(-rows // 128) * 128
    message = 4 if local < 4 else -(-(local + 1) // 8) * 8
    vmem = pl.BlockSpec(memory_space=pltpu.VMEM)
    anywhere = pl.BlockSpec(memory_space=pl.ANY)
    grid, out = pl.pallas_call(
        functools.partial(kernel, n_lat, n_lev),
        out_shape=(
            jax.ShapeDtypeStruct((local, NLON), BF16),
            jax.ShapeDtypeStruct((own, fields, double), BF16),
        ),
        in_specs=[anywhere] * 5,
        out_specs=(vmem, vmem),
        scratch_shapes=[
            pltpu.SMEM(slot_wave.shape, jnp.int32),
            pltpu.SMEM(row_length.shape, jnp.int32),
            pltpu.SMEM(quad_weight.shape, F32),
            pltpu.VMEM((own, fields, double), BF16),
            pltpu.VMEM((own, rows, deg), BF16),
            pltpu.SemaphoreType.DMA((5,)),
            pltpu.VMEM((128, rows_up), F32),
            pltpu.VMEM((rows, 128), F32),
            pltpu.VMEM((n_lat, message, 128), F32),
            pltpu.VMEM((n, message, 128), F32),
            pltpu.VMEM((n, local, 128), F32),
            pltpu.VMEM((n, local, 128), F32),
            pltpu.VMEM((8, NLON), F32),
            pltpu.VMEM((128, rows), F32),
            pltpu.VMEM((local, 4 * HIGH, NLON), BF16),
            pltpu.VMEM((local, 4 * HIGH, NLON), BF16),
            pltpu.VMEM((local, 2 * LOW, NLON), F32),
            pltpu.SemaphoreType.DMA((4,)),
        ],
        compiler_params=pltpu.CompilerParams(
            collective_id=0, has_side_effects=True, vmem_limit_bytes=60 * 1024 * 1024
        ),
    )(
        slot_wave, row_length, quad_weight, spectral_in.reshape(own, fields, double),
        jnp.transpose(legendre.reshape(own, deg, rows), (0, 2, 1)),
    )
    return grid[None], out[None]


def solution(mesh):
    in_specs = (P("lev", "lat", None, None), P("lev", "lat", None, None), P(), P("lat"), P())
    out_specs = (P("lev", "lat", None), P("lev", "lat", None, None))
    body = functools.partial(shards, mesh.shape["lat"], mesh.shape["lev"])
    return jax.shard_map(body, mesh=mesh, in_specs=in_specs, out_specs=out_specs, check_vma=False)
```

```python
import functools

import jax
import jax.numpy as jnp
from jax import lax
from jax.experimental import pallas as pl
from jax.experimental.pallas import tpu as pltpu
from jax.sharding import PartitionSpec as P

M = 640
NLON = 2688
LOW = 32
HIGH = 24
STEP = 896
GROUP = 32
F32 = jnp.float32
BF16 = jnp.bfloat16

SIN = (3.1415927410125732, -5.167709827423096, 2.550076961517334, -0.5982866883277893, 0.07764717191457748)
COS = (1.0, -4.934802055358887, 4.058709144592285, -1.3352116346359253, 0.234935462474823, -0.024393025785684586)


def horner(coefs, x):
    total = jnp.full_like(x, coefs[-1])
    for c in coefs[-2::-1]:
        total = total * x + c
    return total


def turn_cos_sin(product, length):
    inverse = 1.0 / length
    rest = product - jnp.round(product * inverse) * length
    t = rest * inverse
    square = t * t
    half_sin = t * horner(SIN, square)
    half_cos = horner(COS, square)
    return 1.0 - 2.0 * half_sin * half_sin, 2.0 * half_sin * half_cos


def dot_nn(a, b):
    return lax.dot_general(a, b, (((1,), (0,)), ((), ())), preferred_element_type=F32)


def dot_nt(a, b):
    return lax.dot_general(a, b, (((1,), (1,)), ((), ())), preferred_element_type=F32)


def split(x):
    high = x.astype(BF16)
    return high, (x - high.astype(F32)).astype(BF16)


def kernel(
    n_lat, n_lev, wave_in, length_in, quad_in, spec_in, leg_in, grid_ref, out_ref,
    wave_ref, length_ref, quad_ref, spec_ref, leg_ref, load_sems, four, stacked, send1, recv1, send2, recv2, columns, flipped, table_a, table_b, sems,
):
    n = n_lat * n_lev
    lat = lax.axis_index("lat")
    lev = lax.axis_index("lev")
    me = lev * n_lat + lat
    own, fields = spec_ref.shape[0], spec_ref.shape[1]
    rows, deg = leg_ref.shape[1], leg_ref.shape[2]
    local = length_ref.shape[0]
    per_slot = 2 * fields

    def partner(t):
        other = lax.rem(me + t, n)
        return other, (lax.rem(other, n_lat), lax.div(other, n_lat))

    pairs = (
        (spec_in, spec_ref), (leg_in, leg_ref), (wave_in, wave_ref), (length_in, length_ref), (quad_in, quad_ref),
    )
    loads = [pltpu.make_async_copy(src, dst, load_sems.at[i]) for i, (src, dst) in enumerate(pairs)]
    for load in loads:
        load.start()

    barrier = pltpu.get_barrier_semaphore()

    def greet(t, carry):
        pl.semaphore_signal(barrier, inc=1, device_id=partner(t)[1], device_id_type=pl.DeviceIdType.MESH)
        return carry

    lax.fori_loop(1, n, greet, 0)

    loads[3].wait()
    low = lax.broadcasted_iota(jnp.int32, (HIGH + LOW, 128), 0)
    wave = jnp.where(low < HIGH, low * LOW, low - HIGH).astype(F32)
    k = lax.broadcasted_iota(jnp.int32, (HIGH + LOW, 128), 1).astype(F32)
    for r in range(local):
        length = jnp.full((HIGH + LOW, 128), length_ref[r].astype(F32), F32)
        cos_m, sin_m = turn_cos_sin(wave * k, length)
        step_cos, step_sin = turn_cos_sin(wave * 128.0, length)
        for at in range(0, NLON, 128):
            here = pl.ds(at, 128)
            a = jnp.concatenate([cos_m[:HIGH], sin_m[:HIGH]], 0)
            table_a[r, :, here] = jnp.concatenate(split(a), 0)
            table_b[r, :, here] = jnp.concatenate([cos_m[HIGH:], -sin_m[HIGH:]], 0)
            cos_m, sin_m = (
                cos_m * step_cos - sin_m * step_sin,
                sin_m * step_cos + cos_m * step_sin,
            )

    degree = lax.broadcasted_iota(jnp.int32, (per_slot, deg), 1)
    lane = lax.broadcasted_iota(jnp.int32, (1, 128), 1)
    wave_row = jnp.full((1, 128), float(M), F32)
    four[...] = jnp.zeros_like(four)
    for load in loads[:3] + loads[4:]:
        load.wait()
    for s in range(own):
        m = wave_ref[lev, lat * own + s]
        x = spec_ref[s].astype(F32)
        x = jnp.concatenate([x[:, :deg], x[:, deg:]], 0)
        x = jnp.where(degree >= m, x, 0.0).astype(BF16)
        four[pl.ds(s * per_slot, per_slot), pl.ds(0, rows)] = dot_nt(x, leg_ref[s]).astype(BF16).astype(F32)
        wave_row = jnp.where(lane // per_slot == s, m.astype(F32), wave_row)
    turned = four[...].T
    for j in range(n_lat):
        send1[j, pl.ds(0, local), :] = turned[j * local : (j + 1) * local, :]
        send1[j, pl.ds(local, 1), :] = wave_row
        send1[j, pl.ds(local + 1, send1.shape[1] - local - 1), :] = jnp.zeros(
            (send1.shape[1] - local - 1, 128), F32
        )

    pl.semaphore_wait(barrier, n - 1)

    def remote(src, dst, k, device):
        return pltpu.make_async_remote_copy(
            src_ref=src, dst_ref=dst, send_sem=sems.at[2 * k], recv_sem=sems.at[2 * k + 1],
            device_id=device, device_id_type=pl.DeviceIdType.MESH,
        )

    def send_rows(t, carry):
        _, device = partner(t)
        remote(send1.at[device[0]], recv1.at[me], 0, device).start()
        return carry

    lax.fori_loop(1, n, send_rows, 0)
    recv1[me] = send1[lat]

    def all_arrived(buffer, k):
        part = buffer.at[pl.ds(0, n - 1)]
        pltpu.make_async_copy(part, part, sems.at[k]).wait()

    all_arrived(recv1, 1)

    index_a = lax.broadcasted_iota(jnp.int32, (HIGH, 128), 0)
    index_b = lax.broadcasted_iota(jnp.int32, (LOW, 128), 0)
    is_real = lax.rem(lane, per_slot) == lev
    is_imag = lax.rem(lane, per_slot) == lev + fields

    def one_hots(o):
        w = recv1[o, pl.ds(local, 1), :].astype(jnp.int32)
        return index_a == w // LOW, (index_b == w % LOW).astype(F32)

    def place(g, totals):
        lefts = []
        rights = [[] for _ in range(local)]
        for i in range(GROUP):
            o = g * GROUP + i
            hot_a, hot_b = one_hots(o)
            lefts.append(hot_b)
            for r in range(local):
                z = recv1[o, pl.ds(r, 1), :]
                pieces = [
                    jnp.where(hot_a, jnp.where(which, z, 0.0), 0.0) for which in (is_real, is_imag)
                ]
                rights[r].append(jnp.concatenate(pieces, 0))
        left = jnp.concatenate(lefts, 1).astype(BF16)
        right = jnp.concatenate([jnp.concatenate(side, 1) for side in rights], 0).astype(BF16)
        return totals + dot_nt(left, right)

    placed = jnp.zeros((LOW, 2 * HIGH * local), F32)
    placed = place(0, placed) if n == GROUP else lax.fori_loop(0, n // GROUP, place, placed)

    row_b = lax.broadcasted_iota(jnp.int32, (LOW, 2 * HIGH), 0)
    col_a = lax.rem(lax.broadcasted_iota(jnp.int32, (LOW, 2 * HIGH), 1), HIGH)
    factor = jnp.where((row_b == 0) & (col_a == 0), 1.0, 2.0)
    spectra = []
    for r in range(local):
        z = placed[:, 2 * HIGH * r : 2 * HIGH * (r + 1)] * factor
        z_re, z_im = z[:, :HIGH], z[:, HIGH:]
        z = jnp.concatenate(
            [jnp.concatenate([z_re, -z_im] * 2, 1), jnp.concatenate([z_im, z_re] * 2, 1)], 0
        ).astype(BF16)
        length_int = length_ref[r]

        total = jnp.zeros((4 * HIGH, 4 * LOW), F32)
        for at in range(0, NLON, STEP):
            here = pl.ds(at, STEP)
            a = table_a[r, :, here]
            b = table_b[r, :, here]
            raw = jnp.sum(dot_nn(z, a) * b, axis=0, keepdims=True)
            shaped = (raw * (1.0 + 0.5 * jnp.tanh(raw))).astype(BF16).astype(F32)
            k = lax.broadcasted_iota(jnp.int32, (1, STEP), 1) + at
            shaped = jnp.where(k < length_int, shaped, 0.0)
            columns[pl.ds(r, 1), here] = shaped
            total = total + dot_nt(a, jnp.concatenate(split(shaped * b), 0))
        both = 2 * HIGH
        total = total[:both, : 2 * LOW] + total[both:, : 2 * LOW] + total[:both, 2 * LOW :]
        cc, cs = total[:HIGH, :LOW], total[:HIGH, LOW:]
        sc, ss = total[HIGH:, :LOW], total[HIGH:, LOW:]
        length = jnp.full((HIGH, LOW), length_int.astype(F32), F32)
        weight = quad_ref[lat * local + r]
        for part in (cc + ss, cs - sc):
            spectra.append((part / length).astype(BF16).astype(F32) * weight)
    grid_ref[...] = columns[pl.ds(0, local), :].astype(BF16)
    spectrum = jnp.concatenate(spectra, 0).astype(BF16)

    def pick(g, carry):
        hots = [one_hots(g * GROUP + i) for i in range(GROUP)]
        right = jnp.concatenate([hot_b for _, hot_b in hots], 1).astype(BF16)
        spread = dot_nn(spectrum, right)
        for i in range(GROUP):
            cut = spread[:, i * 128 : (i + 1) * 128]
            lines = []
            for r in range(local):
                line = jnp.zeros((1, 128), F32)
                for c, which in enumerate((is_real, is_imag)):
                    first = (2 * r + c) * HIGH
                    value = jnp.sum(
                        jnp.where(hots[i][0], cut[first : first + HIGH], 0.0), axis=0, keepdims=True
                    )
                    line = jnp.where(which, value, line)
                lines.append(line)
            send2[g * GROUP + i] = jnp.concatenate(lines, 0)
        return carry

    if n == GROUP:
        pick(0, 0)
    else:
        lax.fori_loop(0, n // GROUP, pick, 0)

    def send_slots(t, carry):
        other, device = partner(t)
        remote(send2.at[other], recv2.at[me], 1, device).start()
        return carry

    lax.fori_loop(1, n, send_slots, 0)
    recv2[me] = send2[me]
    all_arrived(recv2, 3)

    for j in range(n_lat):
        value = recv2[j]
        for g in range(1, n_lev):
            value = value + recv2[g * n_lat + j]
        stacked[pl.ds(j * local, local), :] = value
    flipped[...] = stacked[...].T
    for s in range(own):
        m = wave_ref[lev, lat * own + s]
        w = flipped[pl.ds(s * per_slot, per_slot), :].astype(BF16)
        y = jnp.where(degree >= m, dot_nn(w, leg_ref[s]), 0.0)
        out_ref[s] = jnp.concatenate([y[:fields], y[fields:]], 1).astype(BF16)

    all_arrived(recv1, 0)
    all_arrived(recv2, 2)


def shards(n_lat, n_lev, spectral_in, legendre, slot_wave, row_length, quad_weight):
    _, own, fields, double = spectral_in.shape
    _, _, deg, rows = legendre.shape
    local = row_length.shape[0]
    n = n_lat * n_lev
    assert fields == n_lev and own * fields * 2 <= 128 and n % GROUP == 0 and rows % 8 == 0
    rows_up = -(-rows // 128) * 128
    message = 4 if local < 4 else -(-(local + 1) // 8) * 8
    vmem = pl.BlockSpec(memory_space=pltpu.VMEM)
    hbm = pl.BlockSpec(memory_space=pltpu.HBM)
    grid, out = pl.pallas_call(
        functools.partial(kernel, n_lat, n_lev),
        out_shape=(
            jax.ShapeDtypeStruct((local, NLON), BF16),
            jax.ShapeDtypeStruct((own, fields, double), BF16),
        ),
        in_specs=[hbm] * 5,
        out_specs=(vmem, vmem),
        scratch_shapes=[
            pltpu.SMEM(slot_wave.shape, jnp.int32),
            pltpu.SMEM(row_length.shape, jnp.int32),
            pltpu.SMEM(quad_weight.shape, F32),
            pltpu.VMEM((own, fields, double), BF16),
            pltpu.VMEM((own, rows, deg), BF16),
            pltpu.SemaphoreType.DMA((5,)),
            pltpu.VMEM((128, rows_up), F32),
            pltpu.VMEM((rows, 128), F32),
            pltpu.VMEM((n_lat, message, 128), F32),
            pltpu.VMEM((n, message, 128), F32),
            pltpu.VMEM((n, local, 128), F32),
            pltpu.VMEM((n, local, 128), F32),
            pltpu.VMEM((8, NLON), F32),
            pltpu.VMEM((128, rows), F32),
            pltpu.VMEM((local, 4 * HIGH, NLON), BF16),
            pltpu.VMEM((local, 2 * LOW, NLON), F32),
            pltpu.SemaphoreType.DMA((4,)),
        ],
        compiler_params=pltpu.CompilerParams(
            collective_id=0, has_side_effects=True, vmem_limit_bytes=55000 * 1024
        ),
    )(
        slot_wave, row_length, quad_weight, spectral_in.reshape(own, fields, double),
        jnp.transpose(legendre.reshape(own, deg, rows), (0, 2, 1)),
    )
    return grid[None], out[None]


def solution(mesh):
    in_specs = (P("lev", "lat", None, None), P("lev", "lat", None, None), P(), P("lat"), P())
    out_specs = (P("lev", "lat", None), P("lev", "lat", None, None))
    body = functools.partial(shards, mesh.shape["lat"], mesh.shape["lev"])
    return jax.shard_map(body, mesh=mesh, in_specs=in_specs, out_specs=out_specs, check_vma=False)
```

```python
import functools

import jax
import jax.numpy as jnp
from jax import lax
from jax.experimental import pallas as pl
from jax.experimental.pallas import tpu as pltpu
from jax.sharding import PartitionSpec as P

M = 640
NLON = 2688
LOW = 32
HIGH = 24
STEP = 896
GROUP = 32
F32 = jnp.float32
BF16 = jnp.bfloat16

SIN = (3.1415927410125732, -5.167709827423096, 2.550076961517334, -0.5982866883277893, 0.07764717191457748)
COS = (1.0, -4.934802055358887, 4.058709144592285, -1.3352116346359253, 0.234935462474823, -0.024393025785684586)


def horner(coefs, x):
    total = jnp.full_like(x, coefs[-1])
    for c in coefs[-2::-1]:
        total = total * x + c
    return total


def turn_cos_sin(product, length):
    inverse = 1.0 / length
    rest = product - jnp.round(product * inverse) * length
    t = rest * inverse
    square = t * t
    half_sin = t * horner(SIN, square)
    half_cos = horner(COS, square)
    return 1.0 - 2.0 * half_sin * half_sin, 2.0 * half_sin * half_cos


def dot_nn(a, b):
    return lax.dot_general(a, b, (((1,), (0,)), ((), ())), preferred_element_type=F32)


def dot_nt(a, b):
    return lax.dot_general(a, b, (((1,), (1,)), ((), ())), preferred_element_type=F32)


def split(x):
    high = x.astype(BF16)
    return high, (x - high.astype(F32)).astype(BF16)


def kernel(
    n_lat, n_lev, wave_in, length_in, quad_in, spec_in, leg_in, grid_ref, out_ref,
    wave_ref, length_ref, quad_ref, spec_ref, leg_ref, load_sems, four, stacked, send1, recv1, send2, recv2, columns, flipped, table_a, table_b, sems,
):
    n = n_lat * n_lev
    lat = lax.axis_index("lat")
    lev = lax.axis_index("lev")
    me = lev * n_lat + lat
    own, fields = spec_ref.shape[0], spec_ref.shape[1]
    rows, deg = leg_ref.shape[1], leg_ref.shape[2]
    local = length_ref.shape[0]
    per_slot = 2 * fields

    def partner(t):
        if isinstance(t, int):
            j = lax.rem(lat + t // n_lev, n_lat) if t >= n_lev else lat
            g = lax.rem(lev + t % n_lev, n_lev) if t % n_lev else lev
        else:
            j, g = lax.rem(lat + t // n_lev, n_lat), lax.rem(lev + t % n_lev, n_lev)
        return g * n_lat + j, (j, g)

    whole = n == GROUP
    partners = [partner(t) for t in range(GROUP)] if whole else None

    def each_partner(act):
        if whole:
            for t in range(1, n):
                act(t, *partners[t])
        else:

            def body(t, carry):
                act(t, *partner(t))
                return carry

            lax.fori_loop(1, n, body, 0)

    pairs = (
        (spec_in, spec_ref), (leg_in, leg_ref), (wave_in, wave_ref), (length_in, length_ref), (quad_in, quad_ref),
    )
    loads = [pltpu.make_async_copy(src, dst, load_sems.at[i]) for i, (src, dst) in enumerate(pairs)]
    for load in loads:
        load.start()

    barrier = pltpu.get_barrier_semaphore()

    def greet(t, other, device):
        pl.semaphore_signal(barrier, inc=1, device_id=device, device_id_type=pl.DeviceIdType.MESH)

    each_partner(greet)

    loads[3].wait()
    low = lax.broadcasted_iota(jnp.int32, (HIGH + LOW, 128), 0)
    wave = jnp.where(low < HIGH, low * LOW, low - HIGH).astype(F32)
    k = lax.broadcasted_iota(jnp.int32, (HIGH + LOW, 128), 1).astype(F32)
    for r in range(local):
        length = jnp.full((HIGH + LOW, 128), length_ref[r].astype(F32), F32)
        cos_m, sin_m = turn_cos_sin(wave * k, length)
        step_cos, step_sin = turn_cos_sin(wave * 128.0, length)
        for at in range(0, NLON, 128):
            here = pl.ds(at, 128)
            a = jnp.concatenate([cos_m[:HIGH], sin_m[:HIGH]], 0)
            table_a[r, :, here] = jnp.concatenate(split(a), 0)
            table_b[r, :, here] = jnp.concatenate([cos_m[HIGH:], -sin_m[HIGH:]], 0)
            cos_m, sin_m = (
                cos_m * step_cos - sin_m * step_sin,
                sin_m * step_cos + cos_m * step_sin,
            )

    degree = lax.broadcasted_iota(jnp.int32, (per_slot, deg), 1)
    lane = lax.broadcasted_iota(jnp.int32, (1, 128), 1)
    wave_row = jnp.full((1, 128), float(M), F32)
    four[...] = jnp.zeros_like(four)
    for load in loads[:3] + loads[4:]:
        load.wait()
    for s in range(own):
        m = wave_ref[lev, lat * own + s]
        x = spec_ref[s].astype(F32)
        x = jnp.concatenate([x[:, :deg], x[:, deg:]], 0)
        x = jnp.where(degree >= m, x, 0.0).astype(BF16)
        four[pl.ds(s * per_slot, per_slot), pl.ds(0, rows)] = dot_nt(x, leg_ref[s]).astype(BF16).astype(F32)
        wave_row = jnp.where(lane // per_slot == s, m.astype(F32), wave_row)
    turned = four[...].T
    for j in range(n_lat):
        send1[j, pl.ds(0, local), :] = turned[j * local : (j + 1) * local, :]
        send1[j, pl.ds(local, 1), :] = wave_row
        send1[j, pl.ds(local + 1, send1.shape[1] - local - 1), :] = jnp.zeros(
            (send1.shape[1] - local - 1, 128), F32
        )

    pl.semaphore_wait(barrier, n - 1)

    def remote(src, dst, k, device):
        return pltpu.make_async_remote_copy(
            src_ref=src, dst_ref=dst, send_sem=sems.at[2 * k], recv_sem=sems.at[2 * k + 1],
            device_id=device, device_id_type=pl.DeviceIdType.MESH,
        )

    def send_rows(t, other, device):
        remote(send1.at[device[0]], recv1.at[me], 0, device).start()

    each_partner(send_rows)
    recv1[me] = send1[lat]

    def all_arrived(buffer, k):
        part = buffer.at[pl.ds(0, n - 1)]
        pltpu.make_async_copy(part, part, sems.at[k]).wait()

    all_arrived(recv1, 1)

    index_a = lax.broadcasted_iota(jnp.int32, (HIGH, 128), 0)
    index_b = lax.broadcasted_iota(jnp.int32, (LOW, 128), 0)
    is_real = lax.rem(lane, per_slot) == lev
    is_imag = lax.rem(lane, per_slot) == lev + fields

    def one_hots(o):
        w = recv1[o, pl.ds(local, 1), :].astype(jnp.int32)
        return index_a == w // LOW, (index_b == w % LOW).astype(F32)

    def place(g, totals):
        lefts = []
        rights = [[] for _ in range(local)]
        for i in range(GROUP):
            o = partners[i][0] if whole else g * GROUP + i
            hot_a, hot_b = one_hots(o)
            lefts.append(hot_b)
            for r in range(local):
                z = recv1[o, pl.ds(r, 1), :]
                pieces = [
                    jnp.where(hot_a, jnp.where(which, z, 0.0), 0.0) for which in (is_real, is_imag)
                ]
                rights[r].append(jnp.concatenate(pieces, 0))
        left = jnp.concatenate(lefts, 1).astype(BF16)
        right = jnp.concatenate([jnp.concatenate(side, 1) for side in rights], 0).astype(BF16)
        return totals + dot_nt(left, right)

    placed = jnp.zeros((LOW, 2 * HIGH * local), F32)
    placed = place(0, placed) if whole else lax.fori_loop(0, n // GROUP, place, placed)

    row_b = lax.broadcasted_iota(jnp.int32, (LOW, 2 * HIGH), 0)
    col_a = lax.rem(lax.broadcasted_iota(jnp.int32, (LOW, 2 * HIGH), 1), HIGH)
    factor = jnp.where((row_b == 0) & (col_a == 0), 1.0, 2.0)
    spectra = []
    for r in range(local):
        z = placed[:, 2 * HIGH * r : 2 * HIGH * (r + 1)] * factor
        z_re, z_im = z[:, :HIGH], z[:, HIGH:]
        z = jnp.concatenate(
            [jnp.concatenate([z_re, -z_im] * 2, 1), jnp.concatenate([z_im, z_re] * 2, 1)], 0
        ).astype(BF16)
        length_int = length_ref[r]

        total = jnp.zeros((4 * HIGH, 4 * LOW), F32)
        for at in range(0, NLON, STEP):
            here = pl.ds(at, STEP)
            a = table_a[r, :, here]
            b = table_b[r, :, here]
            raw = jnp.sum(dot_nn(z, a) * b, axis=0, keepdims=True)
            shaped = (raw * (1.0 + 0.5 * jnp.tanh(raw))).astype(BF16).astype(F32)
            k = lax.broadcasted_iota(jnp.int32, (1, STEP), 1) + at
            shaped = jnp.where(k < length_int, shaped, 0.0)
            columns[pl.ds(r, 1), here] = shaped
            total = total + dot_nt(a, jnp.concatenate(split(shaped * b), 0))
        both = 2 * HIGH
        total = total[:both, : 2 * LOW] + total[both:, : 2 * LOW] + total[:both, 2 * LOW :]
        cc, cs = total[:HIGH, :LOW], total[:HIGH, LOW:]
        sc, ss = total[HIGH:, :LOW], total[HIGH:, LOW:]
        length = jnp.full((HIGH, LOW), length_int.astype(F32), F32)
        weight = quad_ref[lat * local + r]
        for part in (cc + ss, cs - sc):
            spectra.append((part / length).astype(BF16).astype(F32) * weight)
    grid_ref[...] = columns[pl.ds(0, local), :].astype(BF16)
    spectrum = jnp.concatenate(spectra, 0).astype(BF16)

    def pick(g, carry):
        owners = [partners[i][0] if whole else g * GROUP + i for i in range(GROUP)]
        hots = [one_hots(o) for o in owners]
        right = jnp.concatenate([hot_b for _, hot_b in hots], 1).astype(BF16)
        spread = dot_nn(spectrum, right)
        for i in range(GROUP):
            cut = spread[:, i * 128 : (i + 1) * 128]
            lines = []
            for r in range(local):
                line = jnp.zeros((1, 128), F32)
                for c, which in enumerate((is_real, is_imag)):
                    first = (2 * r + c) * HIGH
                    value = jnp.sum(
                        jnp.where(hots[i][0], cut[first : first + HIGH], 0.0), axis=0, keepdims=True
                    )
                    line = jnp.where(which, value, line)
                lines.append(line)
            lines = jnp.concatenate(lines, 0)
            if not whole:
                send2[owners[i]] = lines
            elif i == 0:
                recv2[me] = lines
            else:
                send2[i] = lines
                remote(send2.at[i], recv2.at[me], 1, partners[i][1]).start()
        return carry

    if whole:
        pick(0, 0)
    else:
        lax.fori_loop(0, n // GROUP, pick, 0)

        def send_slots(t, other, device):
            remote(send2.at[other], recv2.at[me], 1, device).start()

        each_partner(send_slots)
        recv2[me] = send2[me]
    all_arrived(recv2, 3)

    for j in range(n_lat):
        value = recv2[j]
        for g in range(1, n_lev):
            value = value + recv2[g * n_lat + j]
        stacked[pl.ds(j * local, local), :] = value
    flipped[...] = stacked[...].T
    for s in range(own):
        m = wave_ref[lev, lat * own + s]
        w = flipped[pl.ds(s * per_slot, per_slot), :].astype(BF16)
        y = jnp.where(degree >= m, dot_nn(w, leg_ref[s]), 0.0)
        out_ref[s] = jnp.concatenate([y[:fields], y[fields:]], 1).astype(BF16)

    all_arrived(recv1, 0)
    all_arrived(recv2, 2)


def shards(n_lat, n_lev, spectral_in, legendre, slot_wave, row_length, quad_weight):
    _, own, fields, double = spectral_in.shape
    _, _, deg, rows = legendre.shape
    local = row_length.shape[0]
    n = n_lat * n_lev
    assert fields == n_lev and own * fields * 2 <= 128 and n % GROUP == 0 and rows % 8 == 0
    rows_up = -(-rows // 128) * 128
    message = 4 if local < 4 else -(-(local + 1) // 8) * 8
    vmem = pl.BlockSpec(memory_space=pltpu.VMEM)
    hbm = pl.BlockSpec(memory_space=pltpu.HBM)
    grid, out = pl.pallas_call(
        functools.partial(kernel, n_lat, n_lev),
        out_shape=(
            jax.ShapeDtypeStruct((local, NLON), BF16),
            jax.ShapeDtypeStruct((own, fields, double), BF16),
        ),
        in_specs=[hbm] * 5,
        out_specs=(vmem, vmem),
        scratch_shapes=[
            pltpu.SMEM(slot_wave.shape, jnp.int32),
            pltpu.SMEM(row_length.shape, jnp.int32),
            pltpu.SMEM(quad_weight.shape, F32),
            pltpu.VMEM((own, fields, double), BF16),
            pltpu.VMEM((own, rows, deg), BF16),
            pltpu.SemaphoreType.DMA((5,)),
            pltpu.VMEM((128, rows_up), F32),
            pltpu.VMEM((rows, 128), F32),
            pltpu.VMEM((n_lat, message, 128), F32),
            pltpu.VMEM((n, message, 128), F32),
            pltpu.VMEM((n, local, 128), F32),
            pltpu.VMEM((n, local, 128), F32),
            pltpu.VMEM((8, NLON), F32),
            pltpu.VMEM((128, rows), F32),
            pltpu.VMEM((local, 4 * HIGH, NLON), BF16),
            pltpu.VMEM((local, 2 * LOW, NLON), F32),
            pltpu.SemaphoreType.DMA((4,)),
        ],
        compiler_params=pltpu.CompilerParams(
            collective_id=0, has_side_effects=True, vmem_limit_bytes=55000 * 1024
        ),
    )(
        slot_wave, row_length, quad_weight, spectral_in.reshape(own, fields, double),
        jnp.transpose(legendre.reshape(own, deg, rows), (0, 2, 1)),
    )
    return grid[None], out[None]


def solution(mesh):
    in_specs = (P("lev", "lat", None, None), P("lev", "lat", None, None), P(), P("lat"), P())
    out_specs = (P("lev", "lat", None), P("lev", "lat", None, None))
    body = functools.partial(shards, mesh.shape["lat"], mesh.shape["lev"])
    return jax.shard_map(body, mesh=mesh, in_specs=in_specs, out_specs=out_specs, check_vma=False)
```

```python
import functools

import jax
import jax.numpy as jnp
from jax import lax
from jax.experimental import pallas as pl
from jax.experimental.pallas import tpu as pltpu
from jax.sharding import PartitionSpec as P

M = 640
NLON = 2688
LOW = 32
HIGH = 24
STEP = 896
GROUP = 32
F32 = jnp.float32
BF16 = jnp.bfloat16

SIN = (3.1415927410125732, -5.167709827423096, 2.550076961517334, -0.5982866883277893, 0.07764717191457748)
COS = (1.0, -4.934802055358887, 4.058709144592285, -1.3352116346359253, 0.234935462474823, -0.024393025785684586)


def horner(coefs, x):
    total = jnp.full_like(x, coefs[-1])
    for c in coefs[-2::-1]:
        total = total * x + c
    return total


def turn_cos_sin(product, length):
    inverse = 1.0 / length
    rest = product - jnp.round(product * inverse) * length
    t = rest * inverse
    square = t * t
    half_sin = t * horner(SIN, square)
    half_cos = horner(COS, square)
    return 1.0 - 2.0 * half_sin * half_sin, 2.0 * half_sin * half_cos


def dot_nn(a, b):
    return lax.dot_general(a, b, (((1,), (0,)), ((), ())), preferred_element_type=F32)


def dot_nt(a, b):
    return lax.dot_general(a, b, (((1,), (1,)), ((), ())), preferred_element_type=F32)


def split(x):
    high = x.astype(BF16)
    return high, (x - high.astype(F32)).astype(BF16)


def kernel(
    n_lat, n_lev, wave_in, length_in, quad_in, spec_in, leg_in, grid_ref, out_ref,
    wave_ref, length_ref, quad_ref, spec_ref, leg_ref, load_sems, four, stacked, send1, recv1, send2, recv2, columns, flipped, table_a, table_b, sems,
):
    n = n_lat * n_lev
    lat = lax.axis_index("lat")
    lev = lax.axis_index("lev")
    me = lev * n_lat + lat
    own, fields = spec_ref.shape[0], spec_ref.shape[1]
    rows, deg = leg_ref.shape[1], leg_ref.shape[2]
    local = length_ref.shape[0]
    per_slot = 2 * fields

    def partner(t):
        if isinstance(t, int):
            j = lax.rem(lat + t // n_lev, n_lat) if t >= n_lev else lat
            g = lax.rem(lev + t % n_lev, n_lev) if t % n_lev else lev
        else:
            j, g = lax.rem(lat + t // n_lev, n_lat), lax.rem(lev + t % n_lev, n_lev)
        return g * n_lat + j, (j, g)

    whole = n == GROUP
    partners = [partner(t) for t in range(GROUP)] if whole else None

    def each_partner(act):
        if whole:
            for t in range(1, n):
                act(t, *partners[t])
        else:

            def body(t, carry):
                act(t, *partner(t))
                return carry

            lax.fori_loop(1, n, body, 0)

    pairs = (
        (spec_in, spec_ref), (leg_in, leg_ref), (wave_in, wave_ref), (length_in, length_ref), (quad_in, quad_ref),
    )
    loads = [pltpu.make_async_copy(src, dst, load_sems.at[i]) for i, (src, dst) in enumerate(pairs)]
    for load in loads:
        load.start()

    barrier = pltpu.get_barrier_semaphore()

    def greet(t, other, device):
        pl.semaphore_signal(barrier, inc=1, device_id=device, device_id_type=pl.DeviceIdType.MESH)

    each_partner(greet)

    loads[3].wait()
    low = lax.broadcasted_iota(jnp.int32, (HIGH + LOW, 128), 0)
    wave = jnp.where(low < HIGH, low * LOW, low - HIGH).astype(F32)
    k = lax.broadcasted_iota(jnp.int32, (HIGH + LOW, 128), 1).astype(F32)
    for r in range(local):
        length = jnp.full((HIGH + LOW, 128), length_ref[r].astype(F32), F32)
        cos_m, sin_m = turn_cos_sin(wave * k, length)
        step_cos, step_sin = turn_cos_sin(wave * 128.0, length)
        for at in range(0, NLON, 128):
            here = pl.ds(at, 128)
            a = jnp.concatenate([cos_m[:HIGH], sin_m[:HIGH]], 0)
            table_a[r, :, here] = jnp.concatenate(split(a), 0)
            table_b[r, :, here] = jnp.concatenate([cos_m[HIGH:], -sin_m[HIGH:]], 0)
            cos_m, sin_m = (
                cos_m * step_cos - sin_m * step_sin,
                sin_m * step_cos + cos_m * step_sin,
            )

    degree = lax.broadcasted_iota(jnp.int32, (per_slot, deg), 1)
    lane = lax.broadcasted_iota(jnp.int32, (1, 128), 1)
    wave_row = jnp.full((1, 128), float(M), F32)
    four[...] = jnp.zeros_like(four)
    for load in loads[:3] + loads[4:]:
        load.wait()
    for s in range(own):
        m = wave_ref[lev, lat * own + s]
        x = spec_ref[s].astype(F32)
        x = jnp.concatenate([x[:, :deg], x[:, deg:]], 0)
        x = jnp.where(degree >= m, x, 0.0).astype(BF16)
        four[pl.ds(s * per_slot, per_slot), pl.ds(0, rows)] = dot_nt(x, leg_ref[s]).astype(BF16).astype(F32)
        wave_row = jnp.where(lane // per_slot == s, m.astype(F32), wave_row)
    turned = four[...].T
    for j in range(n_lat):
        send1[j, pl.ds(0, local), :] = turned[j * local : (j + 1) * local, :]
        send1[j, pl.ds(local, 1), :] = wave_row
        send1[j, pl.ds(local + 1, send1.shape[1] - local - 1), :] = jnp.zeros(
            (send1.shape[1] - local - 1, 128), F32
        )

    pl.semaphore_wait(barrier, n - 1)

    def remote(src, dst, k, device):
        return pltpu.make_async_remote_copy(
            src_ref=src, dst_ref=dst, send_sem=sems.at[2 * k], recv_sem=sems.at[2 * k + 1],
            device_id=device, device_id_type=pl.DeviceIdType.MESH,
        )

    def send_rows(t, other, device):
        remote(send1.at[device[0]], recv1.at[me], 0, device).start()

    each_partner(send_rows)
    recv1[me] = send1[lat]

    def all_arrived(buffer, k):
        part = buffer.at[pl.ds(0, n - 1)]
        pltpu.make_async_copy(part, part, sems.at[k]).wait()

    all_arrived(recv1, 1)

    index_a = lax.broadcasted_iota(jnp.int32, (HIGH, 128), 0)
    index_b = lax.broadcasted_iota(jnp.int32, (LOW, 128), 0)
    is_real = lax.rem(lane, per_slot) == lev
    is_imag = lax.rem(lane, per_slot) == lev + fields

    def one_hots(o):
        w = recv1[o, pl.ds(local, 1), :].astype(jnp.int32)
        return index_a == w // LOW, (index_b == w % LOW).astype(F32)

    def place(g, totals):
        lefts = []
        rights = [[] for _ in range(local)]
        for i in range(GROUP):
            o = partners[i][0] if whole else g * GROUP + i
            hot_a, hot_b = one_hots(o)
            lefts.append(hot_b)
            for r in range(local):
                z = recv1[o, pl.ds(r, 1), :]
                pieces = [
                    jnp.where(hot_a, jnp.where(which, z, 0.0), 0.0) for which in (is_real, is_imag)
                ]
                rights[r].append(jnp.concatenate(pieces, 0))
        left = jnp.concatenate(lefts, 1).astype(BF16)
        right = jnp.concatenate([jnp.concatenate(side, 1) for side in rights], 0).astype(BF16)
        return totals + dot_nt(left, right)

    placed = jnp.zeros((LOW, 2 * HIGH * local), F32)
    placed = place(0, placed) if whole else lax.fori_loop(0, n // GROUP, place, placed)

    row_b = lax.broadcasted_iota(jnp.int32, (LOW, 2 * HIGH), 0)
    col_a = lax.rem(lax.broadcasted_iota(jnp.int32, (LOW, 2 * HIGH), 1), HIGH)
    factor = jnp.where((row_b == 0) & (col_a == 0), 1.0, 2.0)
    spectra = []
    for r in range(local):
        z = placed[:, 2 * HIGH * r : 2 * HIGH * (r + 1)] * factor
        z_re, z_im = z[:, :HIGH], z[:, HIGH:]
        z = jnp.concatenate(
            [jnp.concatenate([z_re, -z_im] * 2, 1), jnp.concatenate([z_im, z_re] * 2, 1)], 0
        ).astype(BF16)
        length_int = length_ref[r]

        total = jnp.zeros((4 * HIGH, 4 * LOW), F32)
        for at in range(0, NLON, STEP):
            here = pl.ds(at, STEP)
            a = table_a[r, :, here]
            b = table_b[r, :, here]
            raw = jnp.sum(dot_nn(z, a) * b, axis=0, keepdims=True)
            shaped = (raw * (1.0 + 0.5 * jnp.tanh(raw))).astype(BF16).astype(F32)
            k = lax.broadcasted_iota(jnp.int32, (1, STEP), 1) + at
            shaped = jnp.where(k < length_int, shaped, 0.0)
            columns[pl.ds(r, 1), here] = shaped
            total = total + dot_nt(a, jnp.concatenate(split(shaped * b), 0))
        both = 2 * HIGH
        total = total[:both, : 2 * LOW] + total[both:, : 2 * LOW] + total[:both, 2 * LOW :]
        cc, cs = total[:HIGH, :LOW], total[:HIGH, LOW:]
        sc, ss = total[HIGH:, :LOW], total[HIGH:, LOW:]
        length = jnp.full((HIGH, LOW), length_int.astype(F32), F32)
        weight = quad_ref[lat * local + r]
        for part in (cc + ss, cs - sc):
            spectra.append((part / length).astype(BF16).astype(F32) * weight)
    grid_ref[...] = columns[pl.ds(0, local), :].astype(BF16)
    spectrum = jnp.concatenate(spectra, 0).astype(BF16)

    def pick(g, carry):
        owners = [partners[i][0] if whole else g * GROUP + i for i in range(GROUP)]
        hots = [one_hots(o) for o in owners]
        right = jnp.concatenate([hot_b for _, hot_b in hots], 1).astype(BF16)
        spread = dot_nn(spectrum, right)
        for i in range(GROUP):
            cut = spread[:, i * 128 : (i + 1) * 128]
            lines = []
            for r in range(local):
                line = jnp.zeros((1, 128), F32)
                for c, which in enumerate((is_real, is_imag)):
                    first = (2 * r + c) * HIGH
                    value = jnp.sum(
                        jnp.where(hots[i][0], cut[first : first + HIGH], 0.0), axis=0, keepdims=True
                    )
                    line = jnp.where(which, value, line)
                lines.append(line)
            lines = jnp.concatenate(lines, 0)
            if not whole:
                send2[owners[i]] = lines
            elif i == 0:
                recv2[me] = lines
            else:
                send2[i] = lines
                remote(send2.at[i], recv2.at[me], 1, partners[i][1]).start()
        return carry

    if whole:
        pick(0, 0)
    else:
        lax.fori_loop(0, n // GROUP, pick, 0)

        def send_slots(t, other, device):
            remote(send2.at[other], recv2.at[me], 1, device).start()

        each_partner(send_slots)
        recv2[me] = send2[me]
    all_arrived(recv2, 3)

    for j in range(n_lat):
        value = recv2[j]
        for g in range(1, n_lev):
            value = value + recv2[g * n_lat + j]
        stacked[pl.ds(j * local, local), :] = value
    flipped[...] = stacked[...].T
    for s in range(own):
        m = wave_ref[lev, lat * own + s]
        w = flipped[pl.ds(s * per_slot, per_slot), :].astype(BF16)
        y = jnp.where(degree >= m, dot_nn(w, leg_ref[s]), 0.0)
        out_ref[s] = jnp.concatenate([y[:fields], y[fields:]], 1).astype(BF16)

    all_arrived(recv1, 0)
    all_arrived(recv2, 2)


def shards(n_lat, n_lev, spectral_in, legendre, slot_wave, row_length, quad_weight):
    _, own, fields, double = spectral_in.shape
    _, _, deg, rows = legendre.shape
    local = row_length.shape[0]
    n = n_lat * n_lev
    assert fields == n_lev and own * fields * 2 <= 128 and n % GROUP == 0 and rows % 8 == 0
    rows_up = -(-rows // 128) * 128
    message = 4 if local < 4 else -(-(local + 1) // 8) * 8
    vmem = pl.BlockSpec(memory_space=pltpu.VMEM)
    hbm = pl.BlockSpec(memory_space=pltpu.HBM)
    grid, out = pl.pallas_call(
        functools.partial(kernel, n_lat, n_lev),
        out_shape=(
            jax.ShapeDtypeStruct((local, NLON), BF16),
            jax.ShapeDtypeStruct((own, fields, double), BF16),
        ),
        in_specs=[hbm] * 5,
        out_specs=(vmem, vmem),
        scratch_shapes=[
            pltpu.SMEM(slot_wave.shape, jnp.int32),
            pltpu.SMEM(row_length.shape, jnp.int32),
            pltpu.SMEM(quad_weight.shape, F32),
            pltpu.VMEM((own, fields, double), BF16),
            pltpu.VMEM((own, rows, deg), BF16),
            pltpu.SemaphoreType.DMA((5,)),
            pltpu.VMEM((128, rows_up), F32),
            pltpu.VMEM((rows, 128), F32),
            pltpu.VMEM((n_lat, message, 128), F32),
            pltpu.VMEM((n, message, 128), F32),
            pltpu.VMEM((n, local, 128), F32),
            pltpu.VMEM((n, local, 128), F32),
            pltpu.VMEM((8, NLON), F32),
            pltpu.VMEM((128, rows), F32),
            pltpu.VMEM((local, 4 * HIGH, NLON), BF16),
            pltpu.VMEM((local, 2 * LOW, NLON), F32),
            pltpu.SemaphoreType.DMA((4,)),
        ],
        compiler_params=pltpu.CompilerParams(
            collective_id=0, has_side_effects=True, vmem_limit_bytes=48 * 1024 * 1024
        ),
    )(*(
        pltpu.with_memory_space_constraint(x, pltpu.HBM)
        for x in (
            slot_wave, row_length, quad_weight, spectral_in.reshape(own, fields, double),
            jnp.transpose(legendre.reshape(own, deg, rows), (0, 2, 1)),
        )
    ))
    return grid[None], out[None]


def solution(mesh):
    in_specs = (P("lev", "lat", None, None), P("lev", "lat", None, None), P(), P("lat"), P())
    out_specs = (P("lev", "lat", None), P("lev", "lat", None, None))
    body = functools.partial(shards, mesh.shape["lat"], mesh.shape["lev"])
    return jax.shard_map(body, mesh=mesh, in_specs=in_specs, out_specs=out_specs, check_vma=False)
```

```python
import functools

import jax
import jax.numpy as jnp
from jax import lax
from jax.experimental import pallas as pl
from jax.experimental.pallas import tpu as pltpu
from jax.sharding import PartitionSpec as P

M = 640
NLON = 2688
LOW = 32
HIGH = 24
STEP = 896
GROUP = 32
F32 = jnp.float32
BF16 = jnp.bfloat16

SIN = (3.1415927410125732, -5.167709827423096, 2.550076961517334, -0.5982866883277893, 0.07764717191457748)
COS = (1.0, -4.934802055358887, 4.058709144592285, -1.3352116346359253, 0.234935462474823, -0.024393025785684586)


def horner(coefs, x):
    total = jnp.full_like(x, coefs[-1])
    for c in coefs[-2::-1]:
        total = total * x + c
    return total


def turn_cos_sin(product, length):
    inverse = 1.0 / length
    rest = product - jnp.round(product * inverse) * length
    t = rest * inverse
    square = t * t
    half_sin = t * horner(SIN, square)
    half_cos = horner(COS, square)
    return 1.0 - 2.0 * half_sin * half_sin, 2.0 * half_sin * half_cos


def dot_nn(a, b):
    return lax.dot_general(a, b, (((1,), (0,)), ((), ())), preferred_element_type=F32)


def dot_nt(a, b):
    return lax.dot_general(a, b, (((1,), (1,)), ((), ())), preferred_element_type=F32)


def split(x):
    high = x.astype(BF16)
    return high, (x - high.astype(F32)).astype(BF16)


def kernel(
    n_lat, n_lev, wave_in, length_in, quad_in, spec_in, leg_in, grid_ref, out_ref,
    wave_ref, length_ref, quad_ref, spec_ref, leg_ref, load_sems, four, stacked, send1, recv1, send2, recv2, columns, flipped, table_a, table_b, sems,
):
    n = n_lat * n_lev
    lat = lax.axis_index("lat")
    lev = lax.axis_index("lev")
    me = lev * n_lat + lat
    own, fields = spec_ref.shape[0], spec_ref.shape[1]
    rows, deg = leg_ref.shape[1], leg_ref.shape[2]
    local = length_ref.shape[0]
    per_slot = 2 * fields

    def partner(t):
        if isinstance(t, int):
            j = lax.rem(lat + t // n_lev, n_lat) if t >= n_lev else lat
            g = lax.rem(lev + t % n_lev, n_lev) if t % n_lev else lev
        else:
            j, g = lax.rem(lat + t // n_lev, n_lat), lax.rem(lev + t % n_lev, n_lev)
        return g * n_lat + j, (j, g)

    whole = n == GROUP
    partners = [partner(t) for t in range(GROUP)] if whole else None

    def each_partner(act):
        if whole:
            for t in range(1, n):
                act(t, *partners[t])
        else:

            def body(t, carry):
                act(t, *partner(t))
                return carry

            lax.fori_loop(1, n, body, 0)

    pairs = (
        (spec_in, spec_ref), (leg_in, leg_ref), (wave_in, wave_ref), (length_in, length_ref), (quad_in, quad_ref),
    )
    loads = [pltpu.make_async_copy(src, dst, load_sems.at[i]) for i, (src, dst) in enumerate(pairs)]
    for load in loads:
        load.start()

    barrier = pltpu.get_barrier_semaphore()

    def greet(t, other, device):
        pl.semaphore_signal(barrier, inc=1, device_id=device, device_id_type=pl.DeviceIdType.MESH)

    each_partner(greet)

    loads[3].wait()
    low = lax.broadcasted_iota(jnp.int32, (HIGH + LOW, 128), 0)
    wave = jnp.where(low < HIGH, low * LOW, low - HIGH).astype(F32)
    k = lax.broadcasted_iota(jnp.int32, (HIGH + LOW, 128), 1).astype(F32)
    for r in range(local):
        length = jnp.full((HIGH + LOW, 128), length_ref[r].astype(F32), F32)
        cos_m, sin_m = turn_cos_sin(wave * k, length)
        step_cos, step_sin = turn_cos_sin(wave * 128.0, length)
        for at in range(0, NLON, 128):
            here = pl.ds(at, 128)
            a = jnp.concatenate([cos_m[:HIGH], sin_m[:HIGH]], 0)
            table_a[r, :, here] = jnp.concatenate(split(a), 0)
            table_b[r, :, here] = jnp.concatenate([cos_m[HIGH:], -sin_m[HIGH:]], 0)
            cos_m, sin_m = (
                cos_m * step_cos - sin_m * step_sin,
                sin_m * step_cos + cos_m * step_sin,
            )

    degree = lax.broadcasted_iota(jnp.int32, (per_slot, deg), 1)
    lane = lax.broadcasted_iota(jnp.int32, (1, 128), 1)
    four[...] = jnp.zeros_like(four)
    for load in loads[:3] + loads[4:]:
        load.wait()
    for s in range(own):
        m = wave_ref[lev, lat * own + s]
        x = spec_ref[s].astype(F32)
        x = jnp.concatenate([x[:, :deg], x[:, deg:]], 0)
        x = jnp.where(degree >= m, x, 0.0).astype(BF16)
        four[pl.ds(s * per_slot, per_slot), pl.ds(0, rows)] = dot_nt(x, leg_ref[s]).astype(BF16).astype(F32)
    turned = four[...].T
    for j in range(n_lat):
        send1[j] = turned[j * local : (j + 1) * local, :]

    pl.semaphore_wait(barrier, n - 1)

    def remote(src, dst, k, device):
        return pltpu.make_async_remote_copy(
            src_ref=src, dst_ref=dst, send_sem=sems.at[2 * k], recv_sem=sems.at[2 * k + 1],
            device_id=device, device_id_type=pl.DeviceIdType.MESH,
        )

    def send_rows(t, other, device):
        remote(send1.at[device[0]], recv1.at[me], 0, device).start()

    each_partner(send_rows)
    recv1[me] = send1[lat]

    def all_arrived(buffer, k):
        part = buffer.at[pl.ds(0, n - 1)]
        pltpu.make_async_copy(part, part, sems.at[k]).wait()

    index_a = lax.broadcasted_iota(jnp.int32, (HIGH, 128), 0)
    index_b = lax.broadcasted_iota(jnp.int32, (LOW, 128), 0)
    is_real = lax.rem(lane, per_slot) == lev
    is_imag = lax.rem(lane, per_slot) == lev + fields
    slot_of = lane // per_slot

    def owners_of(g):
        if whole:
            return partners
        numbers = [g * GROUP + i for i in range(GROUP)]
        return [(o, (lax.rem(o, n_lat), lax.div(o, n_lat))) for o in numbers]

    def one_hots(g):
        highs, lows = [], []
        for _, (j, level) in owners_of(g):
            w = jnp.full((1, 128), M, jnp.int32)
            for s in range(own):
                w = jnp.where(slot_of == s, wave_ref[level, j * own + s], w)
            highs.append(w // LOW)
            lows.append((index_b == w % LOW).astype(F32))
        return highs, jnp.concatenate(lows, 1).astype(BF16)

    ready = one_hots(0) if whole else None

    all_arrived(recv1, 1)

    def place(g, totals):
        highs, left = ready if whole else one_hots(g)
        rights = [[] for _ in range(local)]
        for (o, _), high in zip(owners_of(g), highs):
            hot_a = index_a == high
            for r in range(local):
                z = recv1[o, pl.ds(r, 1), :]
                pieces = [
                    jnp.where(hot_a, jnp.where(which, z, 0.0), 0.0) for which in (is_real, is_imag)
                ]
                rights[r].append(jnp.concatenate(pieces, 0))
        right = jnp.concatenate([jnp.concatenate(side, 1) for side in rights], 0).astype(BF16)
        return totals + dot_nt(left, right)

    placed = jnp.zeros((LOW, 2 * HIGH * local), F32)
    placed = place(0, placed) if whole else lax.fori_loop(0, n // GROUP, place, placed)

    row_b = lax.broadcasted_iota(jnp.int32, (LOW, 2 * HIGH), 0)
    col_a = lax.rem(lax.broadcasted_iota(jnp.int32, (LOW, 2 * HIGH), 1), HIGH)
    factor = jnp.where((row_b == 0) & (col_a == 0), 1.0, 2.0)
    spectra = []
    for r in range(local):
        z = placed[:, 2 * HIGH * r : 2 * HIGH * (r + 1)] * factor
        z_re, z_im = z[:, :HIGH], z[:, HIGH:]
        z = jnp.concatenate(
            [jnp.concatenate([z_re, -z_im] * 2, 1), jnp.concatenate([z_im, z_re] * 2, 1)], 0
        ).astype(BF16)
        length_int = length_ref[r]

        total = jnp.zeros((4 * HIGH, 4 * LOW), F32)
        for at in range(0, NLON, STEP):
            here = pl.ds(at, STEP)
            a = table_a[r, :, here]
            b = table_b[r, :, here]
            raw = jnp.sum(dot_nn(z, a) * b, axis=0, keepdims=True)
            shaped = (raw * (1.0 + 0.5 * jnp.tanh(raw))).astype(BF16).astype(F32)
            k = lax.broadcasted_iota(jnp.int32, (1, STEP), 1) + at
            shaped = jnp.where(k < length_int, shaped, 0.0)
            columns[pl.ds(r, 1), here] = shaped
            total = total + dot_nt(a, jnp.concatenate(split(shaped * b), 0))
        both = 2 * HIGH
        total = total[:both, : 2 * LOW] + total[both:, : 2 * LOW] + total[:both, 2 * LOW :]
        cc, cs = total[:HIGH, :LOW], total[:HIGH, LOW:]
        sc, ss = total[HIGH:, :LOW], total[HIGH:, LOW:]
        length = jnp.full((HIGH, LOW), length_int.astype(F32), F32)
        weight = quad_ref[lat * local + r]
        for part in (cc + ss, cs - sc):
            spectra.append((part / length).astype(BF16).astype(F32) * weight)
    grid_ref[...] = columns[pl.ds(0, local), :].astype(BF16)
    spectrum = jnp.concatenate(spectra, 0).astype(BF16)

    def pick(g, carry):
        owners = [o for o, _ in owners_of(g)]
        highs, right = ready if whole else one_hots(g)
        spread = dot_nn(spectrum, right)
        for i in range(GROUP):
            cut = spread[:, i * 128 : (i + 1) * 128]
            hot_a = index_a == highs[i]
            lines = []
            for r in range(local):
                line = jnp.zeros((1, 128), F32)
                for c, which in enumerate((is_real, is_imag)):
                    first = (2 * r + c) * HIGH
                    value = jnp.sum(
                        jnp.where(hot_a, cut[first : first + HIGH], 0.0), axis=0, keepdims=True
                    )
                    line = jnp.where(which, value, line)
                lines.append(line)
            lines = jnp.concatenate(lines, 0)
            if not whole:
                send2[owners[i]] = lines
            elif i == 0:
                recv2[me] = lines
            else:
                send2[i] = lines
                remote(send2.at[i], recv2.at[me], 1, partners[i][1]).start()
        return carry

    if whole:
        pick(0, 0)
    else:
        lax.fori_loop(0, n // GROUP, pick, 0)

        def send_slots(t, other, device):
            remote(send2.at[other], recv2.at[me], 1, device).start()

        each_partner(send_slots)
        recv2[me] = send2[me]
    all_arrived(recv2, 3)

    for j in range(n_lat):
        value = recv2[j]
        for g in range(1, n_lev):
            value = value + recv2[g * n_lat + j]
        stacked[pl.ds(j * local, local), :] = value
    flipped[...] = stacked[...].T
    for s in range(own):
        m = wave_ref[lev, lat * own + s]
        w = flipped[pl.ds(s * per_slot, per_slot), :].astype(BF16)
        y = jnp.where(degree >= m, dot_nn(w, leg_ref[s]), 0.0)
        out_ref[s] = jnp.concatenate([y[:fields], y[fields:]], 1).astype(BF16)

    all_arrived(recv1, 0)
    all_arrived(recv2, 2)


def shards(n_lat, n_lev, spectral_in, legendre, slot_wave, row_length, quad_weight):
    _, own, fields, double = spectral_in.shape
    _, _, deg, rows = legendre.shape
    local = row_length.shape[0]
    n = n_lat * n_lev
    assert fields == n_lev and own * fields * 2 <= 128 and n % GROUP == 0 and rows % 8 == 0
    rows_up = -(-rows // 128) * 128
    vmem = pl.BlockSpec(memory_space=pltpu.VMEM)
    hbm = pl.BlockSpec(memory_space=pltpu.HBM)
    grid, out = pl.pallas_call(
        functools.partial(kernel, n_lat, n_lev),
        out_shape=(
            jax.ShapeDtypeStruct((local, NLON), BF16),
            jax.ShapeDtypeStruct((own, fields, double), BF16),
        ),
        in_specs=[hbm] * 5,
        out_specs=(vmem, vmem),
        scratch_shapes=[
            pltpu.SMEM(slot_wave.shape, jnp.int32),
            pltpu.SMEM(row_length.shape, jnp.int32),
            pltpu.SMEM(quad_weight.shape, F32),
            pltpu.VMEM((own, fields, double), BF16),
            pltpu.VMEM((own, rows, deg), BF16),
            pltpu.SemaphoreType.DMA((5,)),
            pltpu.VMEM((128, rows_up), F32),
            pltpu.VMEM((rows, 128), F32),
            pltpu.VMEM((n_lat, local, 128), F32),
            pltpu.VMEM((n, local, 128), F32),
            pltpu.VMEM((n, local, 128), F32),
            pltpu.VMEM((n, local, 128), F32),
            pltpu.VMEM((8, NLON), F32),
            pltpu.VMEM((128, rows), F32),
            pltpu.VMEM((local, 4 * HIGH, NLON), BF16),
            pltpu.VMEM((local, 2 * LOW, NLON), F32),
            pltpu.SemaphoreType.DMA((4,)),
        ],
        compiler_params=pltpu.CompilerParams(
            collective_id=0, has_side_effects=True, vmem_limit_bytes=48 * 1024 * 1024
        ),
    )(*(
        pltpu.with_memory_space_constraint(x, pltpu.HBM)
        for x in (
            slot_wave, row_length, quad_weight, spectral_in.reshape(own, fields, double),
            jnp.transpose(legendre.reshape(own, deg, rows), (0, 2, 1)),
        )
    ))
    return grid[None], out[None]


def solution(mesh):
    in_specs = (P("lev", "lat", None, None), P("lev", "lat", None, None), P(), P("lat"), P())
    out_specs = (P("lev", "lat", None), P("lev", "lat", None, None))
    body = functools.partial(shards, mesh.shape["lat"], mesh.shape["lev"])
    return jax.shard_map(body, mesh=mesh, in_specs=in_specs, out_specs=out_specs, check_vma=False)
```

```python
import functools

import jax
import jax.numpy as jnp
from jax import lax
from jax.experimental import pallas as pl
from jax.experimental.pallas import tpu as pltpu
from jax.sharding import PartitionSpec as P

M = 640
NLON = 2688
LOW = 32
HIGH = 24
STEP = 896
GROUP = 32
F32 = jnp.float32
BF16 = jnp.bfloat16

SIN = (3.1415927410125732, -5.167709827423096, 2.550076961517334, -0.5982866883277893, 0.07764717191457748)
COS = (1.0, -4.934802055358887, 4.058709144592285, -1.3352116346359253, 0.234935462474823, -0.024393025785684586)


def horner(coefs, x):
    total = jnp.full_like(x, coefs[-1])
    for c in coefs[-2::-1]:
        total = total * x + c
    return total


def turn_cos_sin(product, length):
    inverse = 1.0 / length
    rest = product - jnp.round(product * inverse) * length
    t = rest * inverse
    square = t * t
    half_sin = t * horner(SIN, square)
    half_cos = horner(COS, square)
    return 1.0 - 2.0 * half_sin * half_sin, 2.0 * half_sin * half_cos


def dot_nn(a, b):
    return lax.dot_general(a, b, (((1,), (0,)), ((), ())), preferred_element_type=F32)


def dot_nt(a, b):
    return lax.dot_general(a, b, (((1,), (1,)), ((), ())), preferred_element_type=F32)


def split(x):
    high = x.astype(BF16)
    return high, (x - high.astype(F32)).astype(BF16)


def kernel(
    n_lat, n_lev, wave_in, length_in, quad_in, spec_in, leg_in, grid_ref, out_ref,
    wave_ref, length_ref, quad_ref, spec_ref, leg_ref, load_sems, four, stacked, send1, recv1, send2, recv2, columns, flipped, table_a, table_b, sems,
):
    n = n_lat * n_lev
    lat = lax.axis_index("lat")
    lev = lax.axis_index("lev")
    me = lev * n_lat + lat
    own, fields = spec_ref.shape[0], spec_ref.shape[1]
    rows, deg = leg_ref.shape[1], leg_ref.shape[2]
    local = length_ref.shape[0]
    per_slot = 2 * fields

    def partner(t):
        if isinstance(t, int):
            j = lax.rem(lat + t // n_lev, n_lat) if t >= n_lev else lat
            g = lax.rem(lev + t % n_lev, n_lev) if t % n_lev else lev
        else:
            j, g = lax.rem(lat + t // n_lev, n_lat), lax.rem(lev + t % n_lev, n_lev)
        return g * n_lat + j, (j, g)

    whole = n == GROUP
    partners = [partner(t) for t in range(GROUP)] if whole else None

    def each_partner(act):
        if whole:
            for t in range(1, n):
                act(t, *partners[t])
        else:

            def body(t, carry):
                act(t, *partner(t))
                return carry

            lax.fori_loop(1, n, body, 0)

    part = own // 3 if own % 3 == 0 else own
    pairs = [(length_in, length_ref), (wave_in, wave_ref), (spec_in, spec_ref)]
    pairs += [(leg_in.at[pl.ds(i, part)], leg_ref.at[pl.ds(i, part)]) for i in range(0, own, part)]
    pairs.append((quad_in, quad_ref))
    loads = [pltpu.make_async_copy(src, dst, load_sems.at[i]) for i, (src, dst) in enumerate(pairs)]
    for load in loads:
        load.start()

    barrier = pltpu.get_barrier_semaphore()

    def greet(t, other, device):
        pl.semaphore_signal(barrier, inc=1, device_id=device, device_id_type=pl.DeviceIdType.MESH)

    each_partner(greet)

    loads[0].wait()
    low = lax.broadcasted_iota(jnp.int32, (HIGH + LOW, 128), 0)
    wave = jnp.where(low < HIGH, low * LOW, low - HIGH).astype(F32)
    k = lax.broadcasted_iota(jnp.int32, (HIGH + LOW, 128), 1).astype(F32)
    for r in range(local):
        length = jnp.full((HIGH + LOW, 128), length_ref[r].astype(F32), F32)
        cos_m, sin_m = turn_cos_sin(wave * k, length)
        step_cos, step_sin = turn_cos_sin(wave * 128.0, length)
        for at in range(0, NLON, 128):
            here = pl.ds(at, 128)
            a = jnp.concatenate([cos_m[:HIGH], sin_m[:HIGH]], 0)
            table_a[r, :, here] = jnp.concatenate(split(a), 0)
            table_b[r, :, here] = jnp.concatenate([cos_m[HIGH:], -sin_m[HIGH:]], 0)
            cos_m, sin_m = (
                cos_m * step_cos - sin_m * step_sin,
                sin_m * step_cos + cos_m * step_sin,
            )

    degree = lax.broadcasted_iota(jnp.int32, (per_slot, deg), 1)
    lane = lax.broadcasted_iota(jnp.int32, (1, 128), 1)
    four[...] = jnp.zeros_like(four)
    loads[1].wait()
    loads[2].wait()
    for s in range(own):
        if s % part == 0:
            loads[3 + s // part].wait()
        m = wave_ref[lev, lat * own + s]
        x = spec_ref[s].astype(F32)
        x = jnp.concatenate([x[:, :deg], x[:, deg:]], 0)
        x = jnp.where(degree >= m, x, 0.0).astype(BF16)
        four[pl.ds(s * per_slot, per_slot), pl.ds(0, rows)] = dot_nt(x, leg_ref[s]).astype(BF16).astype(F32)
    turned = four[...].T
    for j in range(n_lat):
        send1[j] = turned[j * local : (j + 1) * local, :]

    pl.semaphore_wait(barrier, n - 1)

    def remote(src, dst, k, device):
        return pltpu.make_async_remote_copy(
            src_ref=src, dst_ref=dst, send_sem=sems.at[2 * k], recv_sem=sems.at[2 * k + 1],
            device_id=device, device_id_type=pl.DeviceIdType.MESH,
        )

    def send_rows(t, other, device):
        remote(send1.at[device[0]], recv1.at[me], 0, device).start()

    each_partner(send_rows)
    recv1[me] = send1[lat]

    def all_arrived(buffer, k):
        part = buffer.at[pl.ds(0, n - 1)]
        pltpu.make_async_copy(part, part, sems.at[k]).wait()

    index_a = lax.broadcasted_iota(jnp.int32, (HIGH, 128), 0)
    index_b = lax.broadcasted_iota(jnp.int32, (LOW, 128), 0)
    is_real = lax.rem(lane, per_slot) == lev
    is_imag = lax.rem(lane, per_slot) == lev + fields
    slot_of = lane // per_slot

    def owners_of(g):
        if whole:
            return partners
        numbers = [g * GROUP + i for i in range(GROUP)]
        return [(o, (lax.rem(o, n_lat), lax.div(o, n_lat))) for o in numbers]

    def one_hots(g):
        highs, lows = [], []
        for _, (j, level) in owners_of(g):
            w = jnp.full((1, 128), M, jnp.int32)
            for s in range(own):
                w = jnp.where(slot_of == s, wave_ref[level, j * own + s], w)
            highs.append(w // LOW)
            lows.append((index_b == w % LOW).astype(F32))
        return highs, jnp.concatenate(lows, 1).astype(BF16)

    ready = one_hots(0) if whole else None

    loads[-1].wait()
    all_arrived(recv1, 1)

    def place(g, totals):
        highs, left = ready if whole else one_hots(g)
        rights = [[] for _ in range(local)]
        for (o, _), high in zip(owners_of(g), highs):
            hot_a = index_a == high
            for r in range(local):
                z = recv1[o, pl.ds(r, 1), :]
                pieces = [
                    jnp.where(hot_a, jnp.where(which, z, 0.0), 0.0) for which in (is_real, is_imag)
                ]
                rights[r].append(jnp.concatenate(pieces, 0))
        right = jnp.concatenate([jnp.concatenate(side, 1) for side in rights], 0).astype(BF16)
        return totals + dot_nt(left, right)

    placed = jnp.zeros((LOW, 2 * HIGH * local), F32)
    placed = place(0, placed) if whole else lax.fori_loop(0, n // GROUP, place, placed)

    row_b = lax.broadcasted_iota(jnp.int32, (LOW, 2 * HIGH), 0)
    col_a = lax.rem(lax.broadcasted_iota(jnp.int32, (LOW, 2 * HIGH), 1), HIGH)
    factor = jnp.where((row_b == 0) & (col_a == 0), 1.0, 2.0)
    spectra = []
    for r in range(local):
        z = placed[:, 2 * HIGH * r : 2 * HIGH * (r + 1)] * factor
        z_re, z_im = z[:, :HIGH], z[:, HIGH:]
        z = jnp.concatenate(
            [jnp.concatenate([z_re, -z_im] * 2, 1), jnp.concatenate([z_im, z_re] * 2, 1)], 0
        ).astype(BF16)
        length_int = length_ref[r]

        total = jnp.zeros((4 * HIGH, 4 * LOW), F32)
        for at in range(0, NLON, STEP):
            here = pl.ds(at, STEP)
            a = table_a[r, :, here]
            b = table_b[r, :, here]
            raw = jnp.sum(dot_nn(z, a) * b, axis=0, keepdims=True)
            shaped = (raw * (1.0 + 0.5 * jnp.tanh(raw))).astype(BF16).astype(F32)
            k = lax.broadcasted_iota(jnp.int32, (1, STEP), 1) + at
            shaped = jnp.where(k < length_int, shaped, 0.0)
            columns[pl.ds(r, 1), here] = shaped
            total = total + dot_nt(a, jnp.concatenate(split(shaped * b), 0))
        both = 2 * HIGH
        total = total[:both, : 2 * LOW] + total[both:, : 2 * LOW] + total[:both, 2 * LOW :]
        cc, cs = total[:HIGH, :LOW], total[:HIGH, LOW:]
        sc, ss = total[HIGH:, :LOW], total[HIGH:, LOW:]
        length = jnp.full((HIGH, LOW), length_int.astype(F32), F32)
        weight = quad_ref[lat * local + r]
        for part in (cc + ss, cs - sc):
            spectra.append((part / length).astype(BF16).astype(F32) * weight)
    grid_ref[...] = columns[pl.ds(0, local), :].astype(BF16)
    spectrum = jnp.concatenate(spectra, 0).astype(BF16)

    def pick(g, carry):
        owners = [o for o, _ in owners_of(g)]
        highs, right = ready if whole else one_hots(g)
        spread = dot_nn(spectrum, right)
        for i in range(GROUP):
            cut = spread[:, i * 128 : (i + 1) * 128]
            hot_a = index_a == highs[i]
            lines = []
            for r in range(local):
                line = jnp.zeros((1, 128), F32)
                for c, which in enumerate((is_real, is_imag)):
                    first = (2 * r + c) * HIGH
                    value = jnp.sum(
                        jnp.where(hot_a, cut[first : first + HIGH], 0.0), axis=0, keepdims=True
                    )
                    line = jnp.where(which, value, line)
                lines.append(line)
            lines = jnp.concatenate(lines, 0)
            if not whole:
                send2[owners[i]] = lines
            elif i == 0:
                recv2[me] = lines
            else:
                send2[i] = lines
                remote(send2.at[i], recv2.at[me], 1, partners[i][1]).start()
        return carry

    if whole:
        pick(0, 0)
    else:
        lax.fori_loop(0, n // GROUP, pick, 0)

        def send_slots(t, other, device):
            remote(send2.at[other], recv2.at[me], 1, device).start()

        each_partner(send_slots)
        recv2[me] = send2[me]
    all_arrived(recv2, 3)

    for j in range(n_lat):
        value = recv2[j]
        for g in range(1, n_lev):
            value = value + recv2[g * n_lat + j]
        stacked[pl.ds(j * local, local), :] = value
    flipped[...] = stacked[...].T
    for s in range(own):
        m = wave_ref[lev, lat * own + s]
        w = flipped[pl.ds(s * per_slot, per_slot), :].astype(BF16)
        y = jnp.where(degree >= m, dot_nn(w, leg_ref[s]), 0.0)
        out_ref[s] = jnp.concatenate([y[:fields], y[fields:]], 1).astype(BF16)

    all_arrived(recv1, 0)
    all_arrived(recv2, 2)


def shards(n_lat, n_lev, spectral_in, legendre, slot_wave, row_length, quad_weight):
    _, own, fields, double = spectral_in.shape
    _, _, deg, rows = legendre.shape
    local = row_length.shape[0]
    n = n_lat * n_lev
    assert fields == n_lev and own * fields * 2 <= 128 and n % GROUP == 0 and rows % 8 == 0
    rows_up = -(-rows // 128) * 128
    vmem = pl.BlockSpec(memory_space=pltpu.VMEM)
    hbm = pl.BlockSpec(memory_space=pltpu.HBM)
    grid, out = pl.pallas_call(
        functools.partial(kernel, n_lat, n_lev),
        out_shape=(
            jax.ShapeDtypeStruct((local, NLON), BF16),
            jax.ShapeDtypeStruct((own, fields, double), BF16),
        ),
        in_specs=[hbm] * 5,
        out_specs=(vmem, vmem),
        scratch_shapes=[
            pltpu.SMEM(slot_wave.shape, jnp.int32),
            pltpu.SMEM(row_length.shape, jnp.int32),
            pltpu.SMEM(quad_weight.shape, F32),
            pltpu.VMEM((own, fields, double), BF16),
            pltpu.VMEM((own, rows, deg), BF16),
            pltpu.SemaphoreType.DMA((7,)),
            pltpu.VMEM((128, rows_up), F32),
            pltpu.VMEM((rows, 128), F32),
            pltpu.VMEM((n_lat, local, 128), F32),
            pltpu.VMEM((n, local, 128), F32),
            pltpu.VMEM((n, local, 128), F32),
            pltpu.VMEM((n, local, 128), F32),
            pltpu.VMEM((8, NLON), F32),
            pltpu.VMEM((128, rows), F32),
            pltpu.VMEM((local, 4 * HIGH, NLON), BF16),
            pltpu.VMEM((local, 2 * LOW, NLON), F32),
            pltpu.SemaphoreType.DMA((4,)),
        ],
        compiler_params=pltpu.CompilerParams(
            collective_id=0, has_side_effects=True, vmem_limit_bytes=48 * 1024 * 1024
        ),
    )(*(
        pltpu.with_memory_space_constraint(x, pltpu.HBM)
        for x in (
            slot_wave, row_length, quad_weight, spectral_in.reshape(own, fields, double),
            jnp.transpose(legendre.reshape(own, deg, rows), (0, 2, 1)),
        )
    ))
    return grid[None], out[None]


def solution(mesh):
    in_specs = (P("lev", "lat", None, None), P("lev", "lat", None, None), P(), P("lat"), P())
    out_specs = (P("lev", "lat", None), P("lev", "lat", None, None))
    body = functools.partial(shards, mesh.shape["lat"], mesh.shape["lev"])
    return jax.shard_map(body, mesh=mesh, in_specs=in_specs, out_specs=out_specs, check_vma=False)
```
